256 devices in a mesh: query: 8 (over x_hi, y), ref: 32 (over x_lo, z, core).
Axes of the slice: x: 4 (x_hi: 2, x_lo: 2; x = x_hi * 2 + x_lo), y: 4, z: 8, core: 2. Of those that a mesh axis runs over, the one named last changes fastest.
Arguments:
- noise_field: bfloat16 [2048, 12288], P('query'), may hold values from -6 to 6
- ref_crops: bfloat16 [9216, 12288], P('ref'), may hold values from -3 to 3
- level_index: int32 [2048], P('query'), may hold values from 0 to 31
- query_ids: int32 [2048], P('query'), may hold values from 0 to 9215
- w_in: bfloat16 [192, 768], replicated, may hold values from -0.4375 to 0.4375
- bias_hidden: float32 [768], replicated, may hold values from -3 to 3
- w_noise: float32 [768], replicated, may hold values from -4 to 4
- w_out: bfloat16 [768, 192], replicated, may hold values from -0.21875 to 0.21875
Outputs:
- grad_w_in: float32 [192, 768], replicated
- grad_w_out: float32 [768, 192], replicated
- grad_bias: float32 [768], replicated
- grad_noise: float32 [768], replicated
- loss: float32 [], replicated
The draws below stay inside these ranges and needn't reach their ends.
All inputs are finite; a program needn't handle non-finite values.
Results may differ from the reference program's by a relative error of at most 0.0013.
Values may be sent and summed in bfloat16 or wider, within the bound.
A program may use at most 128 MiB of HBM per device.

```python
import jax
import jax.numpy as jnp
from jax import lax

P_SIZE = 192
HID = 768
NLEV = 32
Q_DEV = 256
FEATURES = 12288
QUERIES = 2048
REFS = 9216


def draw_level_index(key, part):
    key = jax.random.fold_in(key, 11)
    shards = QUERIES // Q_DEV
    key_order, key_raw, key_spot = jax.random.split(key, 3)
    order = jax.random.permutation(key_order, shards).astype(jnp.int32)
    kind_of = order % 3
    lower = jnp.where(kind_of == 1, 16, 0).astype(jnp.int32)
    upper = jnp.where(kind_of == 0, 11, NLEV).astype(jnp.int32)
    raw = jax.random.randint(key_raw, (shards, Q_DEV), 0, 1 << 20).astype(jnp.int32)
    level = lower[:, None] + raw % (upper - lower)[:, None]
    spot = jax.random.randint(key_spot, (shards,), 0, Q_DEV).astype(jnp.int32)
    edge = jnp.where(kind_of == 1, NLEV - 1, 0).astype(jnp.int32)
    position = jnp.arange(Q_DEV, dtype=jnp.int32)
    level = jnp.where(position[None, :] == spot[:, None], edge[:, None], level)
    return level.reshape(QUERIES).astype(jnp.int32)


def draw_ref_crops(key, part):
    key = jax.random.fold_in(key, 23)
    key_group, key_base, key_pert = jax.random.split(key, 3)
    groups = jax.random.randint(key_group, (REFS,), 0, 64).astype(jnp.int32)
    base = 0.5 * jax.random.normal(key_base, (64, FEATURES), jnp.float32)
    pert = 0.2 * jax.random.normal(key_pert, (REFS, FEATURES), jnp.float32)
    crops = jnp.take(base, groups, axis=0) + pert
    return jnp.clip(crops, -3.0, 3.0).astype(jnp.bfloat16)


def set_ends(values, stream_key, least, largest):
    dims = values.shape
    index_at = [jax.random.randint(jax.random.fold_in(stream_key, axis), (), 0, dims[axis]) for axis in range(len(dims))]
    values = values.at[tuple(index_at)].set(least)
    longest = dims.index(max(dims))
    index_at[longest] = (index_at[longest] + 1) % dims[longest]
    return values.at[tuple(index_at)].set(largest)


def block_levels(key, extent, cuts, smallest, largest):
    loudness, own = 1.0, jax.random.fold_in(key, 6)
    for axis_at, parts in cuts:
        draws = jnp.exp(jax.random.uniform(jax.random.fold_in(own, axis_at), (parts,), jnp.float32, smallest / len(cuts), largest / len(cuts)))
        loudness = loudness * jnp.repeat(draws, extent[axis_at] // parts).reshape([-1 if axis == axis_at else 1 for axis in range(len(extent))])
    return loudness


def normal_values(key, dims, deviation, limit, cuts=(), kind=jnp.bfloat16):
    entries = jax.random.normal(key, dims, jnp.float32) * deviation
    if len(cuts) > 0:
        entries = block_levels(key, dims, cuts, -0.22, 0.18) * entries
    return jnp.clip(entries, min=-limit, max=limit).astype(kind)


def setup_inputs(seed: int = 0) -> dict:
    seeds = jax.random.split(jax.random.key(seed), 9)
    return {
        "noise_field": normal_values(seeds[0], (QUERIES, FEATURES), 1.0, 6.0, ((0, 8),)),
        "ref_crops": draw_ref_crops(jax.random.fold_in(seeds[8], 71), 0),
        "level_index": draw_level_index(jax.random.fold_in(seeds[8], 71), 0),
        "query_ids": set_ends(jax.random.randint(seeds[3], (QUERIES,), 0, REFS), jax.random.fold_in(seeds[3], 1), 0, REFS - 1).astype(jnp.int32),
        "w_in": normal_values(seeds[4], (P_SIZE, HID), P_SIZE ** -0.5, 0.4375),
        "bias_hidden": normal_values(seeds[5], (HID,), 0.5, 3.0, (), jnp.float32),
        "w_noise": normal_values(seeds[6], (HID,), 1.0, 4.0, (), jnp.float32),
        "w_out": normal_values(seeds[7], (HID, P_SIZE), HID ** -0.5, 0.21875),
    }


sigma_data = 0.5

def noise_level(index):
    low = 0.05 ** (1.0 / 7.0)
    high = 80.0 ** (1.0 / 7.0)
    frac = index.astype(jnp.float32) / (NLEV - 1)
    return (high + frac * (low - high)) ** 7

def tdot(left, right):
    return lax.dot_general(left, right, (((0,), (0,)), ((), ())), preferred_element_type=jnp.float32)

def patch_terms(x_rows, target_rows, sig_rows, w_in, bias_hidden, w_noise, w_out, queries):
    var = sig_rows * sig_rows + sigma_data * sigma_data
    c_skip = sigma_data * sigma_data / var
    c_out = sig_rows * sigma_data / jnp.sqrt(var)
    c_in = 1.0 / jnp.sqrt(var)
    c_noise = jnp.log(sig_rows) / 4.0
    x_full = x_rows.astype(jnp.float32)
    scaled = (c_in[:, None] * x_full).astype(jnp.bfloat16)
    pre = jnp.dot(scaled, w_in, preferred_element_type=jnp.float32) + c_noise[:, None] * w_noise[None, :] + bias_hidden[None, :]
    hidden = jax.nn.silu(pre).astype(jnp.bfloat16)
    output = jnp.dot(hidden, w_out, preferred_element_type=jnp.float32)
    aim = (target_rows - c_skip[:, None] * x_full) / c_out[:, None]
    resid = output - aim
    objective = jnp.sum(resid * resid) / queries
    g_b = (2.0 / queries * resid).astype(jnp.bfloat16)
    g_out = tdot(hidden, g_b)
    back = lax.dot_general(g_b, w_out, (((1,), (1,)), ((), ())), preferred_element_type=jnp.float32)
    sig_p = jax.nn.sigmoid(pre)
    dpre = back * sig_p * (1.0 + pre * (1.0 - sig_p))
    g_in = tdot(scaled, dpre.astype(jnp.bfloat16))
    g_bias = lax.optimization_barrier(jnp.sum(dpre, axis=0))
    g_noise = lax.optimization_barrier(jnp.sum(c_noise[:, None] * dpre, axis=0))
    return (g_in, g_out, g_bias, g_noise, objective)

def reference(noise_field, ref_crops, level_index, query_ids, w_in, bias_hidden, w_noise, w_out):
    queries = noise_field.shape[0]
    feats = noise_field.shape[1]
    ref_sq = lax.optimization_barrier(jnp.sum(jnp.square(ref_crops.astype(jnp.float32)), axis=1))
    block = Q_DEV
    count = queries // block

    def one_block(args):
        noise, levels, ids = args
        clean = jnp.take(ref_crops, ids.astype(jnp.int32), axis=0)
        sigma = noise_level(levels)
        noisy = (clean.astype(jnp.float32) + sigma[:, None] * noise.astype(jnp.float32)).astype(jnp.bfloat16)
        dots = lax.dot_general(noisy, ref_crops, (((1,), (1,)), ((), ())), preferred_element_type=jnp.float32)
        score = (2.0 * dots - ref_sq[None, :]) / (2.0 * sigma[:, None] * sigma[:, None])
        peak = lax.optimization_barrier(jnp.max(score, axis=1))
        weights = jnp.exp(score - peak[:, None]).astype(jnp.bfloat16)
        total = lax.optimization_barrier(jnp.sum(weights.astype(jnp.float32), axis=1))
        acc = jnp.dot(weights, ref_crops, preferred_element_type=jnp.float32)
        target = acc / total[:, None]
        x_rows = noisy.reshape(-1, P_SIZE)
        target_rows = target.reshape(-1, P_SIZE)
        sig_rows = jnp.repeat(sigma, feats // P_SIZE)
        return patch_terms(x_rows, target_rows, sig_rows, w_in, bias_hidden, w_noise, w_out, queries)
    pieces = lax.map(one_block, (noise_field.reshape(count, block, feats), level_index.reshape(count, block), query_ids.reshape(count, block)))
    g_in, g_out, g_bias, g_noise, objective = [lax.optimization_barrier(jnp.sum(p, axis=0)) for p in pieces]
    return (g_in, g_out, g_bias, g_noise, objective / feats)
```

```python
import jax
import jax.numpy as jnp
from jax import lax
from jax.experimental import pallas as pl
from jax.experimental.pallas import tpu as pltpu
from jax.sharding import PartitionSpec as P

NLEV = 32
SIGMA_DATA = 0.5
MESH = pl.DeviceIdType.MESH
F32 = jnp.float32
BF16 = jnp.bfloat16

Z = 8
CHIPS = 2 * Z
Q = 256
HALF = 128
REF = 288
PAIR = 2 * REF
W = 384
PDIM = 192
HID = 768
NQ = 2048
FEATS = 12288


def nt(a, b, **kw):
    return lax.dot_general(a, b, (((1,), (1,)), ((), ())), preferred_element_type=F32, **kw)


def tn(a, b, **kw):
    return lax.dot_general(a, b, (((0,), (0,)), ((), ())), preferred_element_type=F32, **kw)


def nn(a, b):
    return jnp.dot(a, b, preferred_element_type=F32)


def noise_level(index):
    low = 0.05 ** (1.0 / 7.0)
    high = 80.0 ** (1.0 / 7.0)
    frac = index.astype(F32) / (NLEV - 1)
    base = high + frac * (low - high)
    two = base * base
    return two * two * two * base


def column(row):
    return jnp.broadcast_to(row, (128, row.shape[1])).T[:, 0:1]


def row_of(col):
    return jnp.broadcast_to(col, (col.shape[0], 128)).T[0:8]


def main_kernel(
    noise_hbm, refs_hbm, level_ref, ids_ref, w_in_ref, bias_ref, w_noise_ref, w_outT_ref,
    grad_ref,
    refs, prod, match, noisy, noise, dots, halfS, halfR, statS, statR, sqacc,
    axS, axR, azS, azR, bzS, bzR, bxS, bxR, shareS,
    local_sem, swap_ss, swap_rs, half_sem, stat_ss, stat_rs,
    ax_ss, ax_rs, az_ss, az_rs, bz_ss, bz_rs, bx_ss, bx_rs,
    gax_ss, gax_rs, gaz_ss, gaz_rs, gbz_ss, gbz_rs, gbx_ss, gbx_rs,
):
    q = lax.axis_index("query")
    r = lax.axis_index("ref")
    core = r % 2
    chip = r // 2
    z = chip % Z
    xl = chip // Z
    other = 1 - xl

    def at(x_at, z_at, core_at):
        return (x_at * Z + z_at) * 2 + core_at

    sib = at(xl, z, 1 - core)
    xn = at(other, z, core)
    to = (at(xl, (z + Z - 1) % Z, core), at(xl, (z + 1) % Z, core))

    def rcopy(src, dst, ssem, rsem, target):
        return pltpu.make_async_remote_copy(
            src_ref=src, dst_ref=dst, send_sem=ssem, recv_sem=rsem,
            device_id=(q, target), device_id_type=MESH)

    def order(i):
        d = 4 - (i + 1) // 2
        return (z + Z + d * (2 * (i % 2) - 1)) % Z

    def local_copy(b):
        off = pl.multiple_of(core * (FEATS // 2) + b * W, 128)
        return pltpu.make_async_copy(
            refs_hbm.at[:, pl.ds(off, W)], refs.at[b, pl.ds(core * REF, REF), :], local_sem.at[b])

    def swap_copy(b):
        off = pl.multiple_of((1 - core) * (FEATS // 2) + b * W, 128)
        return rcopy(
            refs_hbm.at[:, pl.ds(off, W)], refs.at[b, pl.ds(core * REF, REF), :],
            swap_ss.at[b], swap_rs.at[b], sib)

    def swap_landed(b):
        return rcopy(
            refs_hbm.at[:, pl.ds(0, W)], refs.at[b, pl.ds((1 - core) * REF, REF), :],
            swap_ss.at[b], swap_rs.at[b], sib)

    own = 2 * z + xl

    def start_local(i, _):
        o = order(i)
        local_copy(2 * o).start()
        local_copy(2 * o + 1).start()
        return 0

    lax.fori_loop(0, Z, start_local, 0)
    noise_off = pl.multiple_of(core * (FEATS // 2) + own * W, 128)
    noise_copy = pltpu.make_async_copy(
        noise_hbm.at[:, pl.ds(noise_off, W)], noise, local_sem.at[2 * Z])
    noise_copy.start()

    barrier = pltpu.get_barrier_semaphore()

    def greet(k, _):
        peer = (chip + k) % CHIPS
        pl.semaphore_signal(barrier, inc=1, device_id=(q, peer * 2 + core), device_id_type=MESH)
        return 0

    lax.fori_loop(1, CHIPS, greet, 0)
    pl.semaphore_signal(barrier, inc=1, device_id=(q, sib), device_id_type=MESH)
    pl.semaphore_wait(barrier, CHIPS)

    def start_swap(i, _):
        o = order(i)
        swap_copy(2 * o).start()
        swap_copy(2 * o + 1).start()
        return 0

    lax.fori_loop(0, Z, start_swap, 0)

    sigma = noise_level(level_ref[...])
    sigma_col = column(sigma)
    ids = column(ids_ref[...].astype(F32)) - (chip * PAIR).astype(F32)
    places = lax.broadcasted_iota(jnp.int32, (Q, PAIR), 1).astype(F32)
    match[...] = (ids == places).astype(F32).astype(BF16)

    def reduce_scatter(ph):
        def ax(o):
            return rcopy(axS.at[ph, o], axR.at[ph, o], ax_ss.at[ph, o], ax_rs.at[ph, o], xn)

        def az(d, t):
            if t == 0:
                rows = pl.ds(64 * d, 64)
                return rcopy(azS.at[ph, d, 0, rows], azR.at[ph, d, 0, rows],
                             az_ss.at[ph, d, 0], az_rs.at[ph, d, 0], to[d])
            return rcopy(azS.at[ph, d, t], azR.at[ph, d, t],
                         az_ss.at[ph, d, t], az_rs.at[ph, d, t], to[d])

        def bz(d, t):
            if t == 0:
                return rcopy(bzS.at[ph, d, 0, d], bzR.at[ph, d, 0, d],
                             bz_ss.at[ph, d, 0], bz_rs.at[ph, d, 0], to[d])
            return rcopy(bzS.at[ph, d, t], bzR.at[ph, d, t],
                         bz_ss.at[ph, d, t], bz_rs.at[ph, d, t], to[d])

        def bx():
            return rcopy(bxS.at[ph], bxR.at[ph], bx_ss.at[ph], bx_rs.at[ph], xn)

        def multiply(i, _):
            o = order(i)
            for j in range(2):
                b = 2 * o + j
                if ph == 0:
                    local_copy(b).wait()
                    swap_landed(b).wait_recv()
                prod[b] = nn(match[...], refs[b])
            axS[ph, o] = prod[2 * o + other, 0:HALF].astype(BF16)
            ax(o).start()
            return 0

        multiply(0, 0)
        o = order(0)
        for d in range(2):
            bzS[ph, d, 0, d] = prod[2 * o + d, HALF:Q].astype(BF16)
            bz(d, 0).start()
        lax.fori_loop(1, Z, multiply, 0)

        ax(o).wait_recv()
        for d in range(2):
            rows = slice(64 * d, 64 * d + 64)
            azS[ph, d, 0, rows] = (prod[2 * o + xl, rows] + axR[ph, o, rows].astype(F32)).astype(BF16)
            az(d, 0).start()
        for t in range(1, 4):
            for d in range(2):
                o = (z + Z + (2 * d - 1) * (4 - t)) % Z
                bz(d, t - 1).wait_recv()
                for j in range(2):
                    s = prod[2 * o + j, HALF:Q]
                    if t > 1 or j == d:
                        s = s + bzR[ph, d, t - 1, j].astype(F32)
                    bzS[ph, d, t, j] = s.astype(BF16)
                bz(d, t).start()
            for d in range(2):
                o = (z + Z + (2 * d - 1) * (4 - t)) % Z
                ax(o).wait_recv()
                az(d, t - 1).wait_recv()
                s = prod[2 * o + xl, 0:HALF] + axR[ph, o].astype(F32)
                if t > 1:
                    azS[ph, d, t] = (s + azR[ph, d, t - 1].astype(F32)).astype(BF16)
                else:
                    azS[ph, d, t] = s.astype(BF16)
                    rows = slice(64 * d, 64 * d + 64)
                    azS[ph, d, t, rows] = (s[rows] + azR[ph, d, 0, rows].astype(F32)).astype(BF16)
                az(d, t).start()
        for d in range(2):
            bz(d, 3).wait_recv()
        bxS[ph] = (prod[2 * z + other, HALF:Q] + bzR[ph, 0, 3, other].astype(F32)
                   + bzR[ph, 1, 3, other].astype(F32)).astype(BF16)
        bx().start()
        ax(z).wait_recv()
        for d in range(2):
            az(d, 3).wait_recv()
        top = (prod[own, 0:HALF] + axR[ph, z].astype(F32)
               + azR[ph, 0, 3].astype(F32) + azR[ph, 1, 3].astype(F32))
        bottom = (prod[own, HALF:Q] + bzR[ph, 0, 3, xl].astype(F32)
                  + bzR[ph, 1, 3, xl].astype(F32))
        bx().wait_recv()
        bottom = bottom + bxR[ph].astype(F32)

        def finish():
            for d in range(2):
                for t in range(4):
                    az(d, t).wait_send()
                    bz(d, t).wait_send()
            bx().wait_send()

            def one(o, _):
                ax(o).wait_send()
                return 0

            lax.fori_loop(0, Z, one, 0)

        return top, bottom, finish

    top, bottom, finish0 = reduce_scatter(0)
    noise_copy.wait()
    noisy[own, 0:HALF] = (top + sigma_col[0:HALF] * noise[0:HALF].astype(F32)).astype(BF16)
    noisy[own, HALF:Q] = (bottom + sigma_col[HALF:Q] * noise[HALF:Q].astype(F32)).astype(BF16)

    def same(ref, ssem, rsem, target):
        return rcopy(ref, ref, ssem, rsem, target)

    def gax(o, x_at):
        return same(noisy.at[2 * o + x_at, 0:HALF], gax_ss.at[o], gax_rs.at[o], xn)

    def gbx(x_at):
        return same(noisy.at[2 * z + x_at, HALF:Q], gbx_ss.at[0], gbx_rs.at[0], xn)

    def gaz(d, s, o):
        if s == 4:
            view = noisy.at[2 * o + xl, pl.ds(64 * d, 64)]
        else:
            view = noisy.at[2 * o + xl, 0:HALF]
        return same(view, gaz_ss.at[d, s - 1], gaz_rs.at[d, s - 1], to[d])

    def gbz(d, s, o):
        if s == 4:
            view = noisy.at[2 * o + d, HALF:Q]
        else:
            view = noisy.at[pl.ds(2 * o, 2), HALF:Q]
        return same(view, gbz_ss.at[d, s - 1], gbz_rs.at[d, s - 1], to[d])

    def came(d, s):
        return (z + Z + (1 - 2 * d) * s) % Z

    def score(o, first=False):
        part = nt(noisy[2 * o], refs[2 * o]) + nt(noisy[2 * o + 1], refs[2 * o + 1])
        dots[...] = part if first else dots[...] + part

    gbx(xl).start()
    for d in range(2):
        gaz(d, 1, z).start()
    gax(z, xl).start()
    gbx(other).wait_recv()
    for d in range(2):
        gbz(d, 1, z).start()

    sqacc[...] = jnp.zeros_like(sqacc)

    def squares(b, _):
        v = refs[b].astype(F32)
        v = v * v
        sqacc[...] += v[:, 0:128] + v[:, 128:256] + v[:, 256:384]
        return 0

    lax.fori_loop(0, 2 * Z, squares, 0)

    for s in range(1, 4):
        for d in range(2):
            o = came(d, s)
            gaz(d, s, o).wait_recv()
            gaz(d, s + 1, o).start()
            gax(o, xl).start()
        for d in range(2):
            o = came(d, s)
            gbz(d, s, o).wait_recv()
            gbz(d, s + 1, o).start()
        if s == 1:
            gax(z, other).wait_recv()
            score(z, True)
        else:
            for d in range(2):
                o = came(d, s - 1)
                gax(o, other).wait_recv()
                score(o)
    o = came(0, 4)
    for d in range(2):
        gaz(d, 4, o).wait_recv()
    gax(o, xl).start()
    for d in range(2):
        gax(came(d, 3), other).wait_recv()
        score(came(d, 3))
    for d in range(2):
        gbz(d, 4, o).wait_recv()
    gax(o, other).wait_recv()
    score(o)

    ref_sq = nt(jnp.ones((8, 128), F32), sqacc[...], precision=lax.Precision.HIGHEST)[0:1]
    halfS[...] = 2.0 * dots[...] - ref_sq
    half = rcopy(halfS, halfR, half_sem.at[0], half_sem.at[1], sib)
    half.start()
    half.wait_recv()
    logits = (halfS[...] + halfR[...]) / (2.0 * sigma_col * sigma_col)
    dots[...] = logits

    def stat(i, k):
        peer = ((chip + k) % CHIPS) * 2 + core
        return rcopy(statS.at[i], statR.at[i, k], stat_ss.at[i, k], stat_rs.at[i, k], peer)

    def tell(i, col):
        statS[i] = row_of(col)
        statR[i, 0] = statS[i]

        def one(k, _):
            stat(i, k).start()
            return 0

        lax.fori_loop(1, CHIPS, one, 0)

    def hear(i):
        def one(k, _):
            stat(i, k).wait_recv()
            return 0

        lax.fori_loop(1, CHIPS, one, 0)

    tell(0, jnp.max(logits, axis=1, keepdims=True))
    hear(0)
    peak = column(jnp.max(statR[0], axis=0)[0:1])
    weights = jnp.exp(dots[...] - peak).astype(BF16)
    match[...] = weights
    tell(1, jnp.sum(weights.astype(F32), axis=1, keepdims=True))

    top, bottom, finish1 = reduce_scatter(1)
    shareS[0:HALF] = top
    shareS[HALF:Q] = bottom
    hear(1)
    total = jnp.sum(statR[1], axis=0)[0:1]

    def patches(t):
        return jnp.concatenate([t[0:PDIM], t[PDIM:W]], axis=1)

    def twice(t):
        return jnp.concatenate([t, t], axis=1)

    target = patches(shareS[...].T / total)
    x_full = patches(noisy[own].astype(F32).T)
    s = twice(sigma)
    var = s * s + SIGMA_DATA * SIGMA_DATA
    c_skip = SIGMA_DATA * SIGMA_DATA / var
    c_out = s * SIGMA_DATA / jnp.sqrt(var)
    c_in = 1.0 / jnp.sqrt(var)
    c_noise = jnp.log(s) / 4.0
    scaled = (c_in * x_full).astype(BF16)
    pre = tn(w_in_ref[...], scaled) + column(w_noise_ref[...]) * c_noise + column(bias_ref[...])
    sig_p = jax.nn.sigmoid(pre)
    hidden = (pre * sig_p).astype(BF16)
    resid = nn(w_outT_ref[...], hidden) - (target - c_skip * x_full) / c_out
    objective = jnp.sum(resid * resid) / NQ
    g_b = (2.0 / NQ * resid).astype(BF16)
    g_out = nt(g_b, hidden)
    back = tn(w_outT_ref[...], g_b)
    dpre = back * sig_p * (1.0 + pre * (1.0 - sig_p))
    g_in = nt(scaled, dpre.astype(BF16))
    rows = lax.broadcasted_iota(jnp.int32, (8, 2 * Q), 0)
    pick = jnp.where(rows == 0, 1.0, jnp.where(rows == 1, c_noise, 0.0))
    small = nt(pick, dpre, precision=lax.Precision.HIGHEST)
    small = jnp.where(lax.broadcasted_iota(jnp.int32, (8, HID), 0) == 2, objective, small)
    grad_ref[0:PDIM] = g_in
    grad_ref[PDIM:2 * PDIM] = g_out
    grad_ref[2 * PDIM:2 * PDIM + 8] = small

    finish0()
    finish1()

    def swap_sent(b, _):
        swap_copy(b).wait_send()
        return 0

    lax.fori_loop(0, 2 * Z, swap_sent, 0)
    half.wait_send()

    def stat_sent(k, _):
        stat(0, k).wait_send()
        stat(1, k).wait_send()
        return 0

    lax.fori_loop(1, CHIPS, stat_sent, 0)
    gbx(xl).wait_send()

    def gax_sent(o, _):
        gax(o, xl).wait_send()
        return 0

    lax.fori_loop(0, Z, gax_sent, 0)
    for d in range(2):
        for s in range(1, 5):
            gaz(d, s, z).wait_send()
            gbz(d, s, z).wait_send()


def main_call(noise, refs, level, ids, w_in, bias, w_noise, w_outT):
    dma = pltpu.SemaphoreType.DMA
    vm = pltpu.VMEM
    any_spec = pl.BlockSpec(memory_space=pl.ANY)
    vmem_spec = pl.BlockSpec(memory_space=pltpu.VMEM)
    return pl.pallas_call(
        main_kernel,
        out_shape=jax.ShapeDtypeStruct((2 * PDIM + 8, HID), F32),
        in_specs=[any_spec] * 2 + [vmem_spec] * 6,
        out_specs=vmem_spec,
        scratch_shapes=[
            vm((2 * Z, PAIR, W), BF16),
            vm((2 * Z, Q, W), F32),
            vm((Q, PAIR), BF16),
            vm((2 * Z, Q, W), BF16),
            vm((Q, W), BF16),
            vm((Q, PAIR), F32),
            vm((Q, PAIR), F32),
            vm((Q, PAIR), F32),
            vm((2, 8, Q), F32),
            vm((2, CHIPS, 8, Q), F32),
            vm((PAIR, 128), F32),
            vm((2, Z, HALF, W), BF16),
            vm((2, Z, HALF, W), BF16),
            vm((2, 2, 4, HALF, W), BF16),
            vm((2, 2, 4, HALF, W), BF16),
            vm((2, 2, 4, 2, HALF, W), BF16),
            vm((2, 2, 4, 2, HALF, W), BF16),
            vm((2, HALF, W), BF16),
            vm((2, HALF, W), BF16),
            vm((Q, W), F32),
            dma((2 * Z + 1,)), dma((2 * Z,)), dma((2 * Z,)), dma((2,)),
            dma((2, CHIPS)), dma((2, CHIPS)),
            dma((2, Z)), dma((2, Z)), dma((2, 2, 4)), dma((2, 2, 4)),
            dma((2, 2, 4)), dma((2, 2, 4)), dma((2,)), dma((2,)),
            dma((Z,)), dma((Z,)), dma((2, 4)), dma((2, 4)),
            dma((2, 4)), dma((2, 4)), dma((1,)), dma((1,)),
        ],
        compiler_params=pltpu.CompilerParams(
            collective_id=0, has_side_effects=True, vmem_limit_bytes=56 * 1024 * 1024),
        name="denoise_step",
    )(noise, refs, level, ids, w_in, bias, w_noise, w_outT)


def per_device(noise_field, ref_crops, level_index, query_ids, w_in, bias_hidden, w_noise, w_out):
    grads = main_call(
        noise_field, ref_crops, level_index.reshape(1, Q), query_ids.reshape(1, Q), w_in,
        bias_hidden.reshape(1, HID), w_noise.reshape(1, HID), w_out.T)
    grads = lax.psum(grads, ("query", "ref"))
    g_in = grads[0:PDIM]
    g_out = grads[PDIM:2 * PDIM].T
    small = grads[2 * PDIM:]
    return (g_in, g_out, small[0], small[1], small[2, 0] / FEATS)


def solution(mesh):
    return jax.shard_map(
        per_device,
        mesh=mesh,
        in_specs=(P("query", None), P("ref", None), P("query"), P("query"), P(), P(), P(), P()),
        out_specs=(P(), P(), P(), P(), P()),
        check_vma=False,
    )
```

```python
import jax
import jax.numpy as jnp
from jax import lax
from jax.experimental import pallas as pl
from jax.experimental.pallas import tpu as pltpu
from jax.sharding import PartitionSpec as P

NLEV = 32
SIGMA_DATA = 0.5
MESH = pl.DeviceIdType.MESH
F32 = jnp.float32
BF16 = jnp.bfloat16

Z = 8
CHIPS = 2 * Z
Q = 256
HALF = 128
REF = 288
PAIR = 2 * REF
W = 384
PDIM = 192
HID = 768
NQ = 2048
FEATS = 12288
PLANE = 16
PIECE = 80
OWN = 16
OWNERS = PIECE // OWN


def nt(a, b, **kw):
    return lax.dot_general(a, b, (((1,), (1,)), ((), ())), preferred_element_type=F32, **kw)


def tn(a, b, **kw):
    return lax.dot_general(a, b, (((0,), (0,)), ((), ())), preferred_element_type=F32, **kw)


def nn(a, b):
    return jnp.dot(a, b, preferred_element_type=F32)


def noise_level(index):
    low = 0.05 ** (1.0 / 7.0)
    high = 80.0 ** (1.0 / 7.0)
    frac = index.astype(F32) / (NLEV - 1)
    base = high + frac * (low - high)
    two = base * base
    return two * two * two * base


def column(row):
    return jnp.broadcast_to(row, (128, row.shape[1])).T[:, 0:1]


def row_of(col):
    return jnp.broadcast_to(col, (col.shape[0], 128)).T[0:8]


def main_kernel(
    noise_hbm, refs_hbm, level_ref, ids_ref, w_in_ref, vec_ref, w_outT_ref,
    g_in_ref, g_outT_ref, small_ref,
    grads, coreR, planeS, planeR, zR, whole,
    refs, prod, match, noisy, noise, dots, halfS, halfR, statS, statR, sqacc,
    axS, axR, azS, azR, bzS, bzR, bxS, bxR, shareS,
    local_sem, swap_ss, swap_rs, half_sem, stat_ss, stat_rs,
    ax_ss, ax_rs, az_ss, az_rs, bz_ss, bz_rs, bx_ss, bx_rs,
    gax_ss, gax_rs, gaz_ss, gaz_rs, gbz_ss, gbz_rs, gbx_ss, gbx_rs,
    core_ss, core_rs, plane_ss, plane_rs, z_ss, z_rs, back_ss, back_rs, share_ss, share_rs, swap2_ss, swap2_rs,
):
    q = lax.axis_index("query")
    r = lax.axis_index("ref")
    core = r % 2
    chip = r // 2
    z = chip % Z
    xl = chip // Z
    other = 1 - xl

    def at(x_at, z_at, core_at):
        return (x_at * Z + z_at) * 2 + core_at

    x_hi = q // 4
    y = q % 4
    me = (x_hi * 2 + xl) * 4 + y

    def in_plane(p):
        return ((p // 8) * 4 + p % 4, at((p // 4) % 2, z, core))

    sib = at(xl, z, 1 - core)
    xn = at(other, z, core)
    to = (at(xl, (z + Z - 1) % Z, core), at(xl, (z + 1) % Z, core))

    def rcopy(src, dst, ssem, rsem, target):
        return pltpu.make_async_remote_copy(
            src_ref=src, dst_ref=dst, send_sem=ssem, recv_sem=rsem,
            device_id=(q, target), device_id_type=MESH)

    def order(i):
        d = 4 - (i + 1) // 2
        return (z + Z + d * (2 * (i % 2) - 1)) % Z

    def local_copy(b):
        off = pl.multiple_of(core * (FEATS // 2) + b * W, 128)
        return pltpu.make_async_copy(
            refs_hbm.at[:, pl.ds(off, W)], refs.at[b, pl.ds(core * REF, REF), :], local_sem.at[b])

    def swap_copy(b):
        off = pl.multiple_of((1 - core) * (FEATS // 2) + b * W, 128)
        return rcopy(
            refs_hbm.at[:, pl.ds(off, W)], refs.at[b, pl.ds(core * REF, REF), :],
            swap_ss.at[b], swap_rs.at[b], sib)

    def swap_landed(b):
        return rcopy(
            refs_hbm.at[:, pl.ds(0, W)], refs.at[b, pl.ds((1 - core) * REF, REF), :],
            swap_ss.at[b], swap_rs.at[b], sib)

    own = 2 * z + xl

    def start_local(i, _):
        o = order(i)
        local_copy(2 * o).start()
        local_copy(2 * o + 1).start()
        return 0

    lax.fori_loop(0, Z, start_local, 0)
    noise_off = pl.multiple_of(core * (FEATS // 2) + own * W, 128)
    noise_copy = pltpu.make_async_copy(
        noise_hbm.at[:, pl.ds(noise_off, W)], noise, local_sem.at[2 * Z])
    noise_copy.start()

    barrier = pltpu.get_barrier_semaphore()

    def greet(k, _):
        peer = (chip + k) % CHIPS
        pl.semaphore_signal(barrier, inc=1, device_id=(q, peer * 2 + core), device_id_type=MESH)
        return 0

    lax.fori_loop(1, CHIPS, greet, 0)
    pl.semaphore_signal(barrier, inc=1, device_id=(q, sib), device_id_type=MESH)

    def greet_plane(k, _):
        p = (me + k) % PLANE

        @pl.when(p != x_peer)
        def _():
            pl.semaphore_signal(barrier, inc=1, device_id=in_plane(p), device_id_type=MESH)

        return 0

    x_peer = (x_hi * 2 + other) * 4 + y
    lax.fori_loop(1, PLANE, greet_plane, 0)
    pl.semaphore_wait(barrier, CHIPS + PLANE - 2)

    def start_swap(i, _):
        o = order(i)
        swap_copy(2 * o).start()
        swap_copy(2 * o + 1).start()
        return 0

    lax.fori_loop(0, Z, start_swap, 0)

    sigma = noise_level(level_ref[...])
    sigma_col = column(sigma)
    ids = column(ids_ref[...].astype(F32)) - (chip * PAIR).astype(F32)
    places = lax.broadcasted_iota(jnp.int32, (Q, PAIR), 1).astype(F32)
    match[...] = (ids == places).astype(F32).astype(BF16)

    def reduce_scatter(ph):
        def ax(o):
            return rcopy(axS.at[ph, o], axR.at[ph, o], ax_ss.at[ph, o], ax_rs.at[ph, o], xn)

        def az(d, t):
            if t == 0:
                rows = pl.ds(64 * d, 64)
                return rcopy(azS.at[ph, d, 0, rows], azR.at[ph, d, 0, rows],
                             az_ss.at[ph, d, 0], az_rs.at[ph, d, 0], to[d])
            return rcopy(azS.at[ph, d, t], azR.at[ph, d, t],
                         az_ss.at[ph, d, t], az_rs.at[ph, d, t], to[d])

        def bz(d, t):
            if t == 0:
                return rcopy(bzS.at[ph, d, 0, d], bzR.at[ph, d, 0, d],
                             bz_ss.at[ph, d, 0], bz_rs.at[ph, d, 0], to[d])
            return rcopy(bzS.at[ph, d, t], bzR.at[ph, d, t],
                         bz_ss.at[ph, d, t], bz_rs.at[ph, d, t], to[d])

        def bx():
            return rcopy(bxS.at[ph], bxR.at[ph], bx_ss.at[ph], bx_rs.at[ph], xn)

        def multiply(i, _):
            o = order(i)
            for j in range(2):
                b = 2 * o + j
                if ph == 0:
                    local_copy(b).wait()
                    swap_landed(b).wait_recv()
                prod[b] = nn(match[...], refs[b])
            axS[ph, o] = prod[2 * o + other, 0:HALF].astype(BF16)
            ax(o).start()
            return 0

        multiply(0, 0)
        o = order(0)
        for d in range(2):
            bzS[ph, d, 0, d] = prod[2 * o + d, HALF:Q].astype(BF16)
            bz(d, 0).start()
        lax.fori_loop(1, Z, multiply, 0)

        ax(o).wait_recv()
        for d in range(2):
            rows = slice(64 * d, 64 * d + 64)
            azS[ph, d, 0, rows] = (prod[2 * o + xl, rows] + axR[ph, o, rows].astype(F32)).astype(BF16)
            az(d, 0).start()
        for t in range(1, 4):
            for d in range(2):
                o = (z + Z + (2 * d - 1) * (4 - t)) % Z
                bz(d, t - 1).wait_recv()
                for j in range(2):
                    s = prod[2 * o + j, HALF:Q]
                    if t > 1 or j == d:
                        s = s + bzR[ph, d, t - 1, j].astype(F32)
                    bzS[ph, d, t, j] = s.astype(BF16)
                bz(d, t).start()
            for d in range(2):
                o = (z + Z + (2 * d - 1) * (4 - t)) % Z
                ax(o).wait_recv()
                az(d, t - 1).wait_recv()
                s = prod[2 * o + xl, 0:HALF] + axR[ph, o].astype(F32)
                if t > 1:
                    azS[ph, d, t] = (s + azR[ph, d, t - 1].astype(F32)).astype(BF16)
                else:
                    azS[ph, d, t] = s.astype(BF16)
                    rows = slice(64 * d, 64 * d + 64)
                    azS[ph, d, t, rows] = (s[rows] + azR[ph, d, 0, rows].astype(F32)).astype(BF16)
                az(d, t).start()
        for d in range(2):
            bz(d, 3).wait_recv()
        bxS[ph] = (prod[2 * z + other, HALF:Q] + bzR[ph, 0, 3, other].astype(F32)
                   + bzR[ph, 1, 3, other].astype(F32)).astype(BF16)
        bx().start()
        ax(z).wait_recv()
        for d in range(2):
            az(d, 3).wait_recv()
        top = (prod[own, 0:HALF] + axR[ph, z].astype(F32)
               + azR[ph, 0, 3].astype(F32) + azR[ph, 1, 3].astype(F32))
        bottom = (prod[own, HALF:Q] + bzR[ph, 0, 3, xl].astype(F32)
                  + bzR[ph, 1, 3, xl].astype(F32))
        bx().wait_recv()
        bottom = bottom + bxR[ph].astype(F32)

        def finish():
            for d in range(2):
                for t in range(4):
                    az(d, t).wait_send()
                    bz(d, t).wait_send()
            bx().wait_send()

            def one(o, _):
                ax(o).wait_send()
                return 0

            lax.fori_loop(0, Z, one, 0)

        return top, bottom, finish

    top, bottom, finish0 = reduce_scatter(0)
    noise_copy.wait()
    noisy[own, 0:HALF] = (top + sigma_col[0:HALF] * noise[0:HALF].astype(F32)).astype(BF16)
    noisy[own, HALF:Q] = (bottom + sigma_col[HALF:Q] * noise[HALF:Q].astype(F32)).astype(BF16)

    def same(ref, ssem, rsem, target):
        return rcopy(ref, ref, ssem, rsem, target)

    def gax(o, x_at):
        return same(noisy.at[2 * o + x_at, 0:HALF], gax_ss.at[o], gax_rs.at[o], xn)

    def gbx(x_at):
        return same(noisy.at[2 * z + x_at, HALF:Q], gbx_ss.at[0], gbx_rs.at[0], xn)

    def gaz(d, s, o):
        if s == 4:
            view = noisy.at[2 * o + xl, pl.ds(64 * d, 64)]
        else:
            view = noisy.at[2 * o + xl, 0:HALF]
        return same(view, gaz_ss.at[d, s - 1], gaz_rs.at[d, s - 1], to[d])

    def gbz(d, s, o):
        if s == 4:
            view = noisy.at[2 * o + d, HALF:Q]
        else:
            view = noisy.at[pl.ds(2 * o, 2), HALF:Q]
        return same(view, gbz_ss.at[d, s - 1], gbz_rs.at[d, s - 1], to[d])

    def came(d, s):
        return (z + Z + (1 - 2 * d) * s) % Z

    def score(o, first=False):
        part = nt(noisy[2 * o], refs[2 * o]) + nt(noisy[2 * o + 1], refs[2 * o + 1])
        dots[...] = part if first else dots[...] + part

    gbx(xl).start()
    for d in range(2):
        gaz(d, 1, z).start()
    gax(z, xl).start()
    gbx(other).wait_recv()
    for d in range(2):
        gbz(d, 1, z).start()

    sqacc[...] = jnp.zeros_like(sqacc)

    def squares(b, _):
        v = refs[b].astype(F32)
        v = v * v
        sqacc[...] += v[:, 0:128] + v[:, 128:256] + v[:, 256:384]
        return 0

    lax.fori_loop(0, 2 * Z, squares, 0)

    for s in range(1, 4):
        for d in range(2):
            o = came(d, s)
            gaz(d, s, o).wait_recv()
            gaz(d, s + 1, o).start()
            gax(o, xl).start()
        for d in range(2):
            o = came(d, s)
            gbz(d, s, o).wait_recv()
            gbz(d, s + 1, o).start()
        if s == 1:
            gax(z, other).wait_recv()
            score(z, True)
        else:
            for d in range(2):
                o = came(d, s - 1)
                gax(o, other).wait_recv()
                score(o)
    o = came(0, 4)
    for d in range(2):
        gaz(d, 4, o).wait_recv()
    gax(o, xl).start()
    for d in range(2):
        gax(came(d, 3), other).wait_recv()
        score(came(d, 3))
    for d in range(2):
        gbz(d, 4, o).wait_recv()
    gax(o, other).wait_recv()
    score(o)

    ref_sq = nt(jnp.ones((8, 128), F32), sqacc[...], precision=lax.Precision.HIGHEST)[0:1]
    halfS[...] = 2.0 * dots[...] - ref_sq
    half = rcopy(halfS, halfR, half_sem.at[0], half_sem.at[1], sib)
    half.start()
    half.wait_recv()
    logits = (halfS[...] + halfR[...]) / (2.0 * sigma_col * sigma_col)
    dots[...] = logits

    def stat(i, k):
        peer = ((chip + k) % CHIPS) * 2 + core
        return rcopy(statS.at[i], statR.at[i, k], stat_ss.at[i, k], stat_rs.at[i, k], peer)

    def tell(i, col):
        statS[i] = row_of(col)
        statR[i, 0] = statS[i]

        def one(k, _):
            stat(i, k).start()
            return 0

        lax.fori_loop(1, CHIPS, one, 0)

    def hear(i):
        def one(k, _):
            stat(i, k).wait_recv()
            return 0

        lax.fori_loop(1, CHIPS, one, 0)

    tell(0, jnp.max(logits, axis=1, keepdims=True))
    hear(0)
    peak = column(jnp.max(statR[0], axis=0)[0:1])
    weights = jnp.exp(dots[...] - peak).astype(BF16)
    match[...] = weights
    tell(1, jnp.sum(weights.astype(F32), axis=1, keepdims=True))

    top, bottom, finish1 = reduce_scatter(1)
    shareS[0:HALF] = top
    shareS[HALF:Q] = bottom
    hear(1)
    total = jnp.sum(statR[1], axis=0)[0:1]

    def patches(t):
        return jnp.concatenate([t[0:PDIM], t[PDIM:W]], axis=1)

    def twice(t):
        return jnp.concatenate([t, t], axis=1)

    target = patches(shareS[...].T / total)
    x_full = patches(noisy[own].astype(F32).T)
    s = twice(sigma)
    var = s * s + SIGMA_DATA * SIGMA_DATA
    c_skip = SIGMA_DATA * SIGMA_DATA / var
    c_out = s * SIGMA_DATA / jnp.sqrt(var)
    c_in = 1.0 / jnp.sqrt(var)
    c_noise = jnp.log(s) / 4.0
    scaled = (c_in * x_full).astype(BF16)
    pre = tn(w_in_ref[...], scaled) + column(vec_ref[1:2]) * c_noise + column(vec_ref[0:1])
    sig_p = jax.nn.sigmoid(pre)
    hidden = (pre * sig_p).astype(BF16)
    resid = nn(w_outT_ref[...], hidden) - (target - c_skip * x_full) / c_out
    objective = jnp.sum(resid * resid) / NQ
    g_b = (2.0 / NQ * resid).astype(BF16)
    g_out = nt(g_b, hidden)
    back = tn(w_outT_ref[...], g_b)
    dpre = back * sig_p * (1.0 + pre * (1.0 - sig_p))
    g_in = nt(scaled, dpre.astype(BF16))
    rows = lax.broadcasted_iota(jnp.int32, (8, 2 * Q), 0)
    pick = jnp.where(rows == 0, 1.0, jnp.where(rows == 1, c_noise, 0.0))
    small = nt(pick, dpre, precision=lax.Precision.HIGHEST)
    small = jnp.where(lax.broadcasted_iota(jnp.int32, (8, HID), 0) == 2, objective, small)

    for h in range(2):
        for k in range(3):
            cols = slice(h * W + k * 128, h * W + k * 128 + 128)
            grads[h, k * PDIM:(k + 1) * PDIM] = g_in[:, cols]
            grads[h, (3 + k) * PDIM:(4 + k) * PDIM] = g_out[:, cols]
            grads[h, 6 * PDIM + 8 * k:6 * PDIM + 8 * k + 8] = small[:, cols]
        grads[h, 6 * PDIM + 24:] = jnp.zeros((PLANE * PIECE - 6 * PDIM - 24, 128), F32)

    def piece(p):
        return pl.ds(pl.multiple_of(p * PIECE, 8), PIECE)

    def core_copy(p):
        return rcopy(grads.at[1 - core, piece(p)], coreR.at[piece(p)], core_ss.at[p], core_rs.at[p], sib)

    def plane_copy(k, p):
        return pltpu.make_async_remote_copy(
            src_ref=planeS.at[k], dst_ref=planeR.at[k], send_sem=plane_ss.at[k], recv_sem=plane_rs.at[k],
            device_id=in_plane(p), device_id_type=MESH)

    def start_core(k, _):
        core_copy((me + k) % PLANE).start()
        return 0

    lax.fori_loop(1, PLANE + 1, start_core, 0)

    def start_plane(k, _):
        p = (me + k) % PLANE
        core_copy(p).wait_recv()
        planeS[k] = grads[core, piece(p)] + coreR[piece(p)]
        plane_copy(k, p).start()
        return 0

    lax.fori_loop(1, PLANE, start_plane, 0)
    core_copy(me).wait_recv()
    planeR[0] = grads[core, piece(me)] + coreR[piece(me)]

    def wait_plane(k, _):
        plane_copy(k, (me + k) % PLANE).wait_recv()
        planeR[0] += planeR[k]
        return 0

    lax.fori_loop(1, PLANE, wait_plane, 0)

    def rows_of(o):
        return pl.ds(pl.multiple_of(o * OWN, 8), OWN)

    def z_copy(k, o):
        return rcopy(planeR.at[0, rows_of(o)], zR.at[k], z_ss.at[k], z_rs.at[k], at(xl, o, core))

    def back_copy(k, o):
        view = whole.at[core, me, rows_of(o)]
        return rcopy(view, view, back_ss.at[k], back_rs.at[o], at(xl, (z + k) % Z, core))

    def start_z(k, _):
        o = (z + k) % Z

        @pl.when(o < OWNERS)
        def _():
            z_copy(k, o).start()

        return 0

    lax.fori_loop(1, Z, start_z, 0)

    @pl.when(z < OWNERS)
    def _():
        zR[0] = planeR[0, rows_of(z)]

        def wait_z(k, _):
            z_copy(k, z).wait_recv()
            zR[0] += zR[k]
            return 0

        lax.fori_loop(1, Z, wait_z, 0)
        whole[core, me, rows_of(z)] = zR[0]

        def start_back(k, _):
            back_copy(k, z).start()
            return 0

        lax.fori_loop(1, Z, start_back, 0)

    def wait_back(k, _):
        o = (z + k) % Z

        @pl.when(o < OWNERS)
        def _():
            back_copy(k, o).wait_recv()

        return 0

    lax.fori_loop(1, Z, wait_back, 0)

    def share_copy(k, p, target):
        return pltpu.make_async_remote_copy(
            src_ref=whole.at[core, p], dst_ref=whole.at[core, p], send_sem=share_ss.at[k], recv_sem=share_rs.at[p],
            device_id=in_plane(target), device_id_type=MESH)

    def swap_whole(h, p):
        return rcopy(whole.at[h, p], whole.at[h, p], swap2_ss.at[p], swap2_rs.at[p], sib)

    def start_share(k, _):
        share_copy(k, me, (me + k) % PLANE).start()
        return 0

    lax.fori_loop(1, PLANE, start_share, 0)
    swap_whole(core, me).start()

    def wait_share(k, _):
        p = (me + PLANE - k) % PLANE
        share_copy(k, p, (me + k) % PLANE).wait_recv()
        swap_whole(core, p).start()
        return 0

    lax.fori_loop(1, PLANE, wait_share, 0)

    def wait_swap(p, _):
        swap_whole(1 - core, p).wait_recv()
        return 0

    lax.fori_loop(0, PLANE, wait_swap, 0)
    for h in range(2):
        flat = whole[h].reshape(PLANE * PIECE, 128)
        for k in range(3):
            cols = slice(h * W + k * 128, h * W + k * 128 + 128)
            g_in_ref[:, cols] = flat[k * PDIM:(k + 1) * PDIM]
            g_outT_ref[:, cols] = flat[(3 + k) * PDIM:(4 + k) * PDIM]
            small_ref[:, cols] = flat[6 * PDIM + 8 * k:6 * PDIM + 8 * k + 8]

    def grads_sent(k, _):
        core_copy(k).wait_send()
        swap_whole(core, k).wait_send()
        return 0

    lax.fori_loop(0, PLANE, grads_sent, 0)

    def plane_sent(k, _):
        plane_copy(k, (me + k) % PLANE).wait_send()
        share_copy(k, me, (me + k) % PLANE).wait_send()
        return 0

    lax.fori_loop(1, PLANE, plane_sent, 0)

    def z_sent(k, _):
        o = (z + k) % Z

        @pl.when(o < OWNERS)
        def _():
            z_copy(k, o).wait_send()

        @pl.when(z < OWNERS)
        def _():
            back_copy(k, z).wait_send()

        return 0

    lax.fori_loop(1, Z, z_sent, 0)

    finish0()
    finish1()

    def swap_sent(b, _):
        swap_copy(b).wait_send()
        return 0

    lax.fori_loop(0, 2 * Z, swap_sent, 0)
    half.wait_send()

    def stat_sent(k, _):
        stat(0, k).wait_send()
        stat(1, k).wait_send()
        return 0

    lax.fori_loop(1, CHIPS, stat_sent, 0)
    gbx(xl).wait_send()

    def gax_sent(o, _):
        gax(o, xl).wait_send()
        return 0

    lax.fori_loop(0, Z, gax_sent, 0)
    for d in range(2):
        for s in range(1, 5):
            gaz(d, s, z).wait_send()
            gbz(d, s, z).wait_send()


def main_call(noise, refs, level, ids, w_in, vec, w_outT):
    dma = pltpu.SemaphoreType.DMA
    vm = pltpu.VMEM
    any_spec = pl.BlockSpec(memory_space=pl.ANY)
    vmem_spec = pl.BlockSpec(memory_space=pltpu.VMEM)
    return pl.pallas_call(
        main_kernel,
        out_shape=[
            jax.ShapeDtypeStruct((PDIM, HID), F32),
            jax.ShapeDtypeStruct((PDIM, HID), F32),
            jax.ShapeDtypeStruct((8, HID), F32),
        ],
        in_specs=[any_spec] * 2 + [vmem_spec] * 5,
        out_specs=[vmem_spec] * 3,
        scratch_shapes=[
            vm((2, PLANE * PIECE, 128), F32),
            vm((PLANE * PIECE, 128), F32),
            vm((PLANE, PIECE, 128), F32),
            vm((PLANE, PIECE, 128), F32),
            vm((Z, OWN, 128), F32),
            vm((2, PLANE, PIECE, 128), F32),
            vm((2 * Z, PAIR, W), BF16),
            vm((2 * Z, Q, W), F32),
            vm((Q, PAIR), BF16),
            vm((2 * Z, Q, W), BF16),
            vm((Q, W), BF16),
            vm((Q, PAIR), F32),
            vm((Q, PAIR), F32),
            vm((Q, PAIR), F32),
            vm((2, 8, Q), F32),
            vm((2, CHIPS, 8, Q), F32),
            vm((PAIR, 128), F32),
            vm((2, Z, HALF, W), BF16),
            vm((2, Z, HALF, W), BF16),
            vm((2, 2, 4, HALF, W), BF16),
            vm((2, 2, 4, HALF, W), BF16),
            vm((2, 2, 4, 2, HALF, W), BF16),
            vm((2, 2, 4, 2, HALF, W), BF16),
            vm((2, HALF, W), BF16),
            vm((2, HALF, W), BF16),
            vm((Q, W), F32),
            dma((2 * Z + 1,)), dma((2 * Z,)), dma((2 * Z,)), dma((2,)),
            dma((2, CHIPS)), dma((2, CHIPS)),
            dma((2, Z)), dma((2, Z)), dma((2, 2, 4)), dma((2, 2, 4)),
            dma((2, 2, 4)), dma((2, 2, 4)), dma((2,)), dma((2,)),
            dma((Z,)), dma((Z,)), dma((2, 4)), dma((2, 4)),
            dma((2, 4)), dma((2, 4)), dma((1,)), dma((1,)),
            dma((PLANE,)), dma((PLANE,)), dma((PLANE,)), dma((PLANE,)), dma((Z,)), dma((Z,)),
            dma((Z,)), dma((Z,)), dma((PLANE,)), dma((PLANE,)), dma((PLANE,)), dma((PLANE,)),
        ],
        compiler_params=pltpu.CompilerParams(
            collective_id=0, has_side_effects=True, vmem_limit_bytes=56 * 1024 * 1024),
        name="denoise_step",
    )(noise, refs, level, ids, w_in, vec, w_outT)


def per_device(noise_field, ref_crops, level_index, query_ids, w_in, bias_hidden, w_noise, w_out):
    g_in, g_outT, small = main_call(
        noise_field, ref_crops, level_index.reshape(1, Q), query_ids.reshape(1, Q), w_in,
        jnp.stack([bias_hidden, w_noise]), w_out.T)
    return (g_in, g_outT.T, small[0], small[1], small[2, 0] / FEATS)


def solution(mesh):
    return jax.shard_map(
        per_device,
        mesh=mesh,
        in_specs=(P("query", None), P("ref", None), P("query"), P("query"), P(), P(), P(), P()),
        out_specs=(P(), P(), P(), P(), P()),
        check_vma=False,
    )
```

```python
import jax
import jax.numpy as jnp
from jax import lax
from jax.experimental import pallas as pl
from jax.experimental.pallas import tpu as pltpu
from jax.sharding import PartitionSpec as P

NLEV = 32
SIGMA_DATA = 0.5
MESH = pl.DeviceIdType.MESH
F32 = jnp.float32
BF16 = jnp.bfloat16

Z = 8
CHIPS = 2 * Z
Q = 256
HALF = 128
REF = 288
PAIR = 2 * REF
W = 384
PDIM = 192
HID = 768
NQ = 2048
FEATS = 12288
PLANE = 16
PIECE = 80
OWN = 16
OWNERS = PIECE // OWN


def nt(a, b, **kw):
    return lax.dot_general(a, b, (((1,), (1,)), ((), ())), preferred_element_type=F32, **kw)


def tn(a, b, **kw):
    return lax.dot_general(a, b, (((0,), (0,)), ((), ())), preferred_element_type=F32, **kw)


def nn(a, b):
    return jnp.dot(a, b, preferred_element_type=F32)


def noise_level(index):
    low = 0.05 ** (1.0 / 7.0)
    high = 80.0 ** (1.0 / 7.0)
    frac = index.astype(F32) / (NLEV - 1)
    base = high + frac * (low - high)
    two = base * base
    return two * two * two * base


def column(row):
    return jnp.broadcast_to(row, (128, row.shape[1])).T[:, 0:1]


def row_of(col):
    return jnp.broadcast_to(col, (col.shape[0], 128)).T[0:8]


def main_kernel(
    noise_hbm, refs_hbm, level_ref, ids_ref, w_in_hbm, bias_ref, w_noise_ref, w_outT_hbm,
    g_in_ref, g_outT_ref, small_ref,
    grads, coreR, planeS, planeR, zR, whole,
    w_in_ref, w_outT_ref, scaled_ref, slope_ref, hidden_ref, fit_ref,
    refs, prod, match, noisy, noise, dots, halfS, halfR, statS, statR, sqacc,
    xS, xR, zS, zR2, idsR, match2,
    axS, axR, azS, azR, bzS, bzR, bxS, bxR, shareS,
    local_sem, swap_ss, swap_rs, half_sem, stat_ss, stat_rs,
    x_ss, x_rs, zz_ss, zz_rs, ids_sem,
    ax_ss, ax_rs, az_ss, az_rs, bz_ss, bz_rs, bx_ss, bx_rs,
    gax_ss, gax_rs, gaz_ss, gaz_rs, gbz_ss, gbz_rs, gbx_ss, gbx_rs,
    core_ss, core_rs, plane_ss, plane_rs, z_ss, z_rs, back_ss, back_rs, share_ss, share_rs, swap2_ss, swap2_rs,
):
    q = lax.axis_index("query")
    r = lax.axis_index("ref")
    core = r % 2
    chip = r // 2
    z = chip % Z
    xl = chip // Z
    other = 1 - xl

    def at(x_at, z_at, core_at):
        return (x_at * Z + z_at) * 2 + core_at

    x_hi = q // 4
    y = q % 4
    me = (x_hi * 2 + xl) * 4 + y

    def in_plane(p):
        return ((p // 8) * 4 + p % 4, at((p // 4) % 2, z, core))

    sib = at(xl, z, 1 - core)
    xn = at(other, z, core)
    to = (at(xl, (z + Z - 1) % Z, core), at(xl, (z + 1) % Z, core))

    def rcopy(src, dst, ssem, rsem, target):
        return pltpu.make_async_remote_copy(
            src_ref=src, dst_ref=dst, send_sem=ssem, recv_sem=rsem,
            device_id=(q, target), device_id_type=MESH)

    def order(i):
        d = 4 - (i + 1) // 2
        return (z + Z + d * (2 * (i % 2) - 1)) % Z

    def local_copy(b):
        off = pl.multiple_of(core * (FEATS // 2) + b * W, 128)
        return pltpu.make_async_copy(
            refs_hbm.at[:, pl.ds(off, W)], refs.at[b, pl.ds(core * REF, REF), :], local_sem.at[b])

    def swap_copy(b):
        off = pl.multiple_of((1 - core) * (FEATS // 2) + b * W, 128)
        return rcopy(
            refs_hbm.at[:, pl.ds(off, W)], refs.at[b, pl.ds(core * REF, REF), :],
            swap_ss.at[b], swap_rs.at[b], sib)

    def swap_landed(b):
        return rcopy(
            refs_hbm.at[:, pl.ds(0, W)], refs.at[b, pl.ds((1 - core) * REF, REF), :],
            swap_ss.at[b], swap_rs.at[b], sib)

    own = 2 * z + xl

    def start_local(i, _):
        o = order(i)
        local_copy(2 * o).start()
        local_copy(2 * o + 1).start()
        return 0

    lax.fori_loop(0, Z, start_local, 0)
    noise_off = pl.multiple_of(core * (FEATS // 2) + own * W, 128)
    noise_copy = pltpu.make_async_copy(
        noise_hbm.at[:, pl.ds(noise_off, W)], noise, local_sem.at[2 * Z])
    noise_copy.start()
    w_in_copy = pltpu.make_async_copy(w_in_hbm, w_in_ref, local_sem.at[2 * Z + 1])
    w_out_copy = pltpu.make_async_copy(w_outT_hbm, w_outT_ref, local_sem.at[2 * Z + 2])
    w_in_copy.start()
    w_out_copy.start()

    barrier = pltpu.get_barrier_semaphore()

    def greet(k, _):
        peer = (chip + k) % CHIPS
        pl.semaphore_signal(barrier, inc=1, device_id=(q, peer * 2 + core), device_id_type=MESH)
        return 0

    lax.fori_loop(1, CHIPS, greet, 0)
    pl.semaphore_signal(barrier, inc=1, device_id=(q, sib), device_id_type=MESH)

    def greet_plane(k, _):
        p = (me + k) % PLANE

        @pl.when(p != x_peer)
        def _():
            pl.semaphore_signal(barrier, inc=1, device_id=in_plane(p), device_id_type=MESH)

        return 0

    x_peer = (x_hi * 2 + other) * 4 + y
    lax.fori_loop(1, PLANE, greet_plane, 0)
    pl.semaphore_wait(barrier, CHIPS + PLANE - 2)

    sent = []

    def start_swap(i):
        o = order(i)
        swap_copy(2 * o).start()
        swap_copy(2 * o + 1).start()

    xo = at(other, z, core)
    q_xo = (1 - x_hi) * 4 + y
    ids_copy = pltpu.make_async_remote_copy(
        src_ref=ids_ref, dst_ref=idsR, send_sem=ids_sem.at[0], recv_sem=ids_sem.at[1],
        device_id=(q_xo, xo), device_id_type=MESH)
    ids_copy.start()
    sent.append(ids_copy.wait_send)
    for i in range(3):
        start_swap(i)

    def swap_sent():
        def one(b, _):
            swap_copy(b).wait_send()
            return 0

        lax.fori_loop(0, 2 * Z, one, 0)

    sent.append(swap_sent)

    sigma = noise_level(level_ref[...])
    sigma_col = column(sigma)
    places = lax.broadcasted_iota(jnp.int32, (Q, PAIR), 1).astype(F32)

    def one_hot(row):
        ids = column(row.astype(F32)) - (chip * PAIR).astype(F32)
        return (ids == places).astype(F32).astype(BF16)

    match[...] = one_hot(ids_ref[...])
    match2[0:HALF] = match[0:HALF]

    def x_copy(side, o):
        return pltpu.make_async_remote_copy(
            src_ref=xS.at[side, o], dst_ref=xR.at[side, o], send_sem=x_ss.at[side, o], recv_sem=x_rs.at[side, o],
            device_id=(q if side == 0 else q_xo, xn), device_id_type=MESH)

    def z_step(d, t):
        rows = pl.ds(HALF * d, HALF) if t == 0 else slice(None)
        return rcopy(zS.at[d, t, rows], zR2.at[d, t, rows], zz_ss.at[d, t], zz_rs.at[d, t], to[d])

    def first_multiply(i):
        o = order(i)
        if i + 3 < Z:
            start_swap(i + 3)
        for j in range(2):
            local_copy(2 * o + j).wait()
            swap_landed(2 * o + j).wait_recv()
        part = nn(match2[...], refs[2 * o + other]).astype(BF16)
        for side in range(2):
            xS[side, o] = part[side * HALF:(side + 1) * HALF]
            x_copy(side, o).start()
        prod[2 * o + xl] = nn(match[...], refs[2 * o + xl])

    def first_sum(o, side):
        x_copy(side, o).wait_recv()
        return prod[2 * o + xl, side * HALF:(side + 1) * HALF] + xR[side, o].astype(F32)

    def toward(d, t):
        return (z + Z + (2 * d - 1) * (4 - t)) % Z

    def first_reduce(idle):
        for i in range(3):
            first_multiply(i)
        for d in range(2):
            zS[d, 0, d * HALF:(d + 1) * HALF] = first_sum(toward(d, 0), d).astype(BF16)
            z_step(d, 0).start()
        for t in range(1, 4):
            for i in range(2 * t + 1, min(2 * t + 3, Z)):
                first_multiply(i)
            idle(t)
            for d in range(2):
                z_step(d, t - 1).wait_recv()
                for side in range(2):
                    rows = slice(side * HALF, (side + 1) * HALF)
                    part = first_sum(toward(d, t), side)
                    if t > 1 or side == d:
                        part = part + zR2[d, t - 1, rows].astype(F32)
                    zS[d, t, rows] = part.astype(BF16)
                z_step(d, t).start()
        idle(0)
        parts = [first_sum(z, side) for side in range(2)]
        for d in range(2):
            z_step(d, 3).wait_recv()
            for side in range(2):
                parts[side] = parts[side] + zR2[d, 3, side * HALF:(side + 1) * HALF].astype(F32)

        def finish():
            for d in range(2):
                for t in range(4):
                    z_step(d, t).wait_send()

            def one(o, _):
                x_copy(0, o).wait_send()
                x_copy(1, o).wait_send()
                return 0

            lax.fori_loop(0, Z, one, 0)

        sent.append(finish)
        return parts

    def reduce_scatter(idle):
        def ax(o):
            return rcopy(axS.at[o], axR.at[o], ax_ss.at[o], ax_rs.at[o], xn)

        def az(d, t):
            rows = pl.ds(64 * d, 64) if t == 0 else slice(None)
            return rcopy(azS.at[d, t, rows], azR.at[d, t, rows], az_ss.at[d, t], az_rs.at[d, t], to[d])

        def bz(d, t):
            if t == 0:
                return rcopy(bzS.at[d, 0, d], bzR.at[d, 0, d], bz_ss.at[d, 0], bz_rs.at[d, 0], to[d])
            return rcopy(bzS.at[d, t], bzR.at[d, t], bz_ss.at[d, t], bz_rs.at[d, t], to[d])

        def bx():
            return rcopy(bxS, bxR, bx_ss.at[0], bx_rs.at[0], xn)

        def multiply(i):
            o = order(i)
            for j in range(2):
                prod[2 * o + j] = nn(match[...], refs[2 * o + j])
            axS[o] = prod[2 * o + other, 0:HALF].astype(BF16)
            ax(o).start()

        multiply(0)
        for d in range(2):
            bzS[d, 0, d] = prod[2 * toward(d, 0) + d, HALF:Q].astype(BF16)
            bz(d, 0).start()
        multiply(1)
        multiply(2)
        idle(0)
        o = toward(0, 0)
        ax(o).wait_recv()
        for d in range(2):
            rows = slice(64 * d, 64 * d + 64)
            azS[d, 0, rows] = (prod[2 * o + xl, rows] + axR[o, rows].astype(F32)).astype(BF16)
            az(d, 0).start()
        for t in range(1, 4):
            for d in range(2):
                o = toward(d, t)
                bz(d, t - 1).wait_recv()
                for j in range(2):
                    s = prod[2 * o + j, HALF:Q]
                    if t > 1 or j == d:
                        s = s + bzR[d, t - 1, j].astype(F32)
                    bzS[d, t, j] = s.astype(BF16)
                bz(d, t).start()
            for i in range(2 * t + 1, min(2 * t + 3, Z)):
                multiply(i)
            for d in range(2):
                o = toward(d, t)
                ax(o).wait_recv()
                az(d, t - 1).wait_recv()
                s = prod[2 * o + xl, 0:HALF] + axR[o].astype(F32)
                if t > 1:
                    azS[d, t] = (s + azR[d, t - 1].astype(F32)).astype(BF16)
                else:
                    azS[d, t] = s.astype(BF16)
                    rows = slice(64 * d, 64 * d + 64)
                    azS[d, t, rows] = (s[rows] + azR[d, 0, rows].astype(F32)).astype(BF16)
                az(d, t).start()
            idle(t)
        for d in range(2):
            bz(d, 3).wait_recv()
        bxS[...] = (prod[2 * z + other, HALF:Q] + bzR[0, 3, other].astype(F32)
                    + bzR[1, 3, other].astype(F32)).astype(BF16)
        bx().start()
        ax(z).wait_recv()
        for d in range(2):
            az(d, 3).wait_recv()
        top = (prod[own, 0:HALF] + axR[z].astype(F32) + azR[0, 3].astype(F32) + azR[1, 3].astype(F32))
        bottom = prod[own, HALF:Q] + bzR[0, 3, xl].astype(F32) + bzR[1, 3, xl].astype(F32)
        bx().wait_recv()
        bottom = bottom + bxR[...].astype(F32)

        def finish():
            for d in range(2):
                for t in range(4):
                    az(d, t).wait_send()
                    bz(d, t).wait_send()
            bx().wait_send()

            def one(o, _):
                ax(o).wait_send()
                return 0

            lax.fori_loop(0, Z, one, 0)

        sent.append(finish)
        return top, bottom

    sqacc[...] = jnp.zeros_like(sqacc)

    def squares(t):
        def one(b, _):
            v = refs[b].astype(F32)
            v = v * v
            sqacc[...] += v[:, 0:128] + v[:, 128:256] + v[:, 256:384]
            return 0

        if t == 0:
            lax.fori_loop(0, 2 * Z, one, 0)

    ids_copy.wait_recv()
    match2[HALF:Q] = one_hot(idsR[...])[HALF:Q]
    top, bottom = first_reduce(squares)
    noise_copy.wait()
    noisy[own, 0:HALF] = (top + sigma_col[0:HALF] * noise[0:HALF].astype(F32)).astype(BF16)
    noisy[own, HALF:Q] = (bottom + sigma_col[HALF:Q] * noise[HALF:Q].astype(F32)).astype(BF16)

    def same(ref, ssem, rsem, target):
        return rcopy(ref, ref, ssem, rsem, target)

    def gax(o, x_at):
        return same(noisy.at[2 * o + x_at, 0:HALF], gax_ss.at[o], gax_rs.at[o], xn)

    def gbx(x_at):
        return same(noisy.at[2 * z + x_at, HALF:Q], gbx_ss.at[0], gbx_rs.at[0], xn)

    def gaz(d, s, o):
        if s == 4:
            view = noisy.at[2 * o + xl, pl.ds(64 * d, 64)]
        else:
            view = noisy.at[2 * o + xl, 0:HALF]
        return same(view, gaz_ss.at[d, s - 1], gaz_rs.at[d, s - 1], to[d])

    def gbz(d, s, o):
        if s == 4:
            view = noisy.at[2 * o + d, HALF:Q]
        else:
            view = noisy.at[pl.ds(2 * o, 2), HALF:Q]
        return same(view, gbz_ss.at[d, s - 1], gbz_rs.at[d, s - 1], to[d])

    def came(d, s):
        return (z + Z + (1 - 2 * d) * s) % Z

    def score(o, first=False):
        part = nt(noisy[2 * o], refs[2 * o]) + nt(noisy[2 * o + 1], refs[2 * o + 1])
        dots[...] = part if first else dots[...] + part

    gbx(xl).start()
    for d in range(2):
        gaz(d, 1, z).start()
    gax(z, xl).start()
    gbx(other).wait_recv()
    for d in range(2):
        gbz(d, 1, z).start()

    for s in range(1, 4):
        for d in range(2):
            o = came(d, s)
            gaz(d, s, o).wait_recv()
            gaz(d, s + 1, o).start()
            gax(o, xl).start()
        for d in range(2):
            o = came(d, s)
            gbz(d, s, o).wait_recv()
            gbz(d, s + 1, o).start()
        if s == 1:
            gax(z, other).wait_recv()
            score(z, True)
        else:
            for d in range(2):
                o = came(d, s - 1)
                gax(o, other).wait_recv()
                score(o)
    ref_sq = nt(jnp.ones((8, 128), F32), sqacc[...], precision=lax.Precision.HIGHEST)[0:1]
    o = came(0, 4)
    for d in range(2):
        gaz(d, 4, o).wait_recv()
    gax(o, xl).start()
    for d in range(2):
        gax(came(d, 3), other).wait_recv()
        score(came(d, 3))
    for d in range(2):
        gbz(d, 4, o).wait_recv()
    gax(o, other).wait_recv()
    score(o)

    def gather_sent():
        gbx(xl).wait_send()

        def one(o, _):
            gax(o, xl).wait_send()
            return 0

        lax.fori_loop(0, Z, one, 0)
        for d in range(2):
            for s in range(1, 5):
                gaz(d, s, z).wait_send()
                gbz(d, s, z).wait_send()

    sent.append(gather_sent)

    halfS[...] = 2.0 * dots[...] - ref_sq
    half = rcopy(halfS, halfR, half_sem.at[0], half_sem.at[1], sib)
    half.start()
    sent.append(half.wait_send)
    half.wait_recv()
    logits = (halfS[...] + halfR[...]) / (2.0 * sigma_col * sigma_col)
    dots[...] = logits

    def stat(i, k):
        peer = ((chip + k) % CHIPS) * 2 + core
        return rcopy(statS.at[i], statR.at[i, k], stat_ss.at[i, k], stat_rs.at[i, k], peer)

    def tell(i, col):
        statS[i] = row_of(col)[0:1]
        statR[i, 0] = statS[i]

        def one(k, _):
            stat(i, k).start()
            return 0

        lax.fori_loop(1, CHIPS, one, 0)

        def told():
            def one(k, _):
                stat(i, k).wait_send()
                return 0

            lax.fori_loop(1, CHIPS, one, 0)

        sent.append(told)

    def hear(i):
        def one(k, _):
            stat(i, k).wait_recv()
            return 0

        lax.fori_loop(1, CHIPS, one, 0)

    mine = jnp.max(logits, axis=1, keepdims=True)
    tell(0, mine)
    dots[...] = jnp.exp(logits - mine)
    hear(0)
    peak = column(jnp.max(statR[0], axis=0))
    match[...] = (dots[...] * jnp.exp(mine - peak)).astype(BF16)

    def patches(t):
        return jnp.concatenate([t[0:PDIM], t[PDIM:W]], axis=1)

    def twice(t):
        return jnp.concatenate([t, t], axis=1)

    s = twice(sigma)
    var = s * s + SIGMA_DATA * SIGMA_DATA
    c_skip = SIGMA_DATA * SIGMA_DATA / var
    c_out = s * SIGMA_DATA / jnp.sqrt(var)
    c_in = 1.0 / jnp.sqrt(var)
    c_noise = jnp.log(s) / 4.0

    def forward(t):
        if t == 0:
            tell(1, jnp.sum(match[...].astype(F32), axis=1, keepdims=True))
            w_in_copy.wait()
            w_out_copy.wait()
        elif t == 1:
            x_full = patches(noisy[own].astype(F32).T)
            scaled = (c_in * x_full).astype(BF16)
            scaled_ref[...] = scaled
            fit_ref[...] = c_skip * x_full / c_out
            slope_ref[...] = (tn(w_in_ref[...], scaled) + column(w_noise_ref[...].reshape(1, HID)) * c_noise
                              + column(bias_ref[...].reshape(1, HID)))
        elif t == 2:
            pre = slope_ref[...]
            sig_p = jax.nn.sigmoid(pre)
            hidden_ref[...] = (pre * sig_p).astype(BF16)
            slope_ref[...] = sig_p * (1.0 + pre * (1.0 - sig_p))
        else:
            fit_ref[...] += nn(w_outT_ref[...], hidden_ref[...])

    top, bottom = reduce_scatter(forward)
    shareS[0:HALF] = top
    shareS[HALF:Q] = bottom
    hear(1)
    total = jnp.sum(statR[1], axis=0)

    resid = fit_ref[...] - patches(shareS[...].T / total) / c_out
    g_b = (2.0 / NQ * resid).astype(BF16)

    def strips(at_row, value):
        rows = value.shape[0]
        for h in range(2):
            for k in range(3):
                cols = slice(h * W + k * 128, h * W + k * 128 + 128)
                grads[h, at_row + k * rows:at_row + (k + 1) * rows] = value[:, cols]

    def piece(p):
        return pl.ds(pl.multiple_of(p * PIECE, 8), PIECE)

    def core_copy(p):
        return rcopy(grads.at[1 - core, piece(p)], coreR.at[piece(p)], core_ss.at[p], core_rs.at[p], sib)

    def start_core(p, _):
        core_copy(p).start()
        return 0

    early = 3 * PDIM // PIECE
    strips(0, nt(g_b, hidden_ref[...]))
    lax.fori_loop(0, early, start_core, 0)
    dpre = tn(w_outT_ref[...], g_b) * slope_ref[...]
    strips(3 * PDIM, nt(scaled_ref[...], dpre.astype(BF16)))
    objective = jnp.sum(resid * resid) / NQ
    rows = lax.broadcasted_iota(jnp.int32, (8, 2 * Q), 0)
    pick = jnp.where(rows == 0, 1.0, jnp.where(rows == 1, c_noise, 0.0))
    small = nt(pick, dpre, precision=lax.Precision.HIGHEST)
    strips(6 * PDIM, jnp.where(lax.broadcasted_iota(jnp.int32, (8, HID), 0) == 2, objective, small))
    for h in range(2):
        grads[h, 6 * PDIM + 24:] = jnp.zeros((PLANE * PIECE - 6 * PDIM - 24, 128), F32)
    lax.fori_loop(early, PLANE, start_core, 0)

    def plane_copy(k, p):
        return pltpu.make_async_remote_copy(
            src_ref=planeS.at[k], dst_ref=planeR.at[k], send_sem=plane_ss.at[k], recv_sem=plane_rs.at[k],
            device_id=in_plane(p), device_id_type=MESH)

    def start_plane(k, _):
        p = (me + k) % PLANE
        core_copy(p).wait_recv()
        planeS[k] = grads[core, piece(p)] + coreR[piece(p)]
        plane_copy(k, p).start()
        return 0

    lax.fori_loop(1, PLANE, start_plane, 0)
    core_copy(me).wait_recv()
    planeR[0] = grads[core, piece(me)] + coreR[piece(me)]

    def wait_plane(k, _):
        plane_copy(k, (me + k) % PLANE).wait_recv()
        planeR[0] += planeR[k]
        return 0

    lax.fori_loop(1, PLANE, wait_plane, 0)

    def rows_of(o):
        return pl.ds(pl.multiple_of(o * OWN, 8), OWN)

    def z_copy(k, o):
        return rcopy(planeR.at[0, rows_of(o)], zR.at[k], z_ss.at[k], z_rs.at[k], at(xl, o, core))

    def back_copy(k, o):
        view = whole.at[core, me, rows_of(o)]
        return rcopy(view, view, back_ss.at[k], back_rs.at[o], at(xl, (z + k) % Z, core))

    def start_z(k, _):
        o = (z + k) % Z

        @pl.when(o < OWNERS)
        def _():
            z_copy(k, o).start()

        return 0

    lax.fori_loop(1, Z, start_z, 0)

    @pl.when(z < OWNERS)
    def _():
        zR[0] = planeR[0, rows_of(z)]

        def wait_z(k, _):
            z_copy(k, z).wait_recv()
            zR[0] += zR[k]
            return 0

        lax.fori_loop(1, Z, wait_z, 0)
        whole[core, me, rows_of(z)] = zR[0]

        def start_back(k, _):
            back_copy(k, z).start()
            return 0

        lax.fori_loop(1, Z, start_back, 0)

    def wait_back(k, _):
        o = (z + k) % Z

        @pl.when(o < OWNERS)
        def _():
            back_copy(k, o).wait_recv()

        return 0

    lax.fori_loop(1, Z, wait_back, 0)

    def share_copy(k, p, target):
        return pltpu.make_async_remote_copy(
            src_ref=whole.at[core, p], dst_ref=whole.at[core, p], send_sem=share_ss.at[k], recv_sem=share_rs.at[p],
            device_id=in_plane(target), device_id_type=MESH)

    def swap_whole(h, p):
        return rcopy(whole.at[h, p], whole.at[h, p], swap2_ss.at[p], swap2_rs.at[p], sib)

    def start_share(k, _):
        share_copy(k, me, (me + k) % PLANE).start()
        return 0

    lax.fori_loop(1, PLANE, start_share, 0)
    swap_whole(core, me).start()

    def wait_share(k, _):
        p = (me + PLANE - k) % PLANE
        share_copy(k, p, (me + k) % PLANE).wait_recv()
        swap_whole(core, p).start()
        return 0

    lax.fori_loop(1, PLANE, wait_share, 0)

    def wait_swap(p, _):
        swap_whole(1 - core, p).wait_recv()
        return 0

    lax.fori_loop(0, PLANE, wait_swap, 0)
    for h in range(2):
        flat = whole[h].reshape(PLANE * PIECE, 128)
        for k in range(3):
            cols = slice(h * W + k * 128, h * W + k * 128 + 128)
            g_outT_ref[:, cols] = flat[k * PDIM:(k + 1) * PDIM]
            g_in_ref[:, cols] = flat[(3 + k) * PDIM:(4 + k) * PDIM]
            small_ref[:, cols] = flat[6 * PDIM + 8 * k:6 * PDIM + 8 * k + 8]

    def grads_sent(k, _):
        core_copy(k).wait_send()
        swap_whole(core, k).wait_send()
        return 0

    lax.fori_loop(0, PLANE, grads_sent, 0)

    def plane_sent(k, _):
        plane_copy(k, (me + k) % PLANE).wait_send()
        share_copy(k, me, (me + k) % PLANE).wait_send()
        return 0

    lax.fori_loop(1, PLANE, plane_sent, 0)

    def z_sent(k, _):
        o = (z + k) % Z

        @pl.when(o < OWNERS)
        def _():
            z_copy(k, o).wait_send()

        @pl.when(z < OWNERS)
        def _():
            back_copy(k, z).wait_send()

        return 0

    lax.fori_loop(1, Z, z_sent, 0)

    for wait in sent:
        wait()


def main_call(noise, refs, level, ids, w_in, bias, w_noise, w_outT):
    dma = pltpu.SemaphoreType.DMA
    vm = pltpu.VMEM
    any_spec = pl.BlockSpec(memory_space=pl.ANY)
    vmem_spec = pl.BlockSpec(memory_space=pltpu.VMEM)
    return pl.pallas_call(
        main_kernel,
        out_shape=[
            jax.ShapeDtypeStruct((PDIM, HID), F32),
            jax.ShapeDtypeStruct((PDIM, HID), F32),
            jax.ShapeDtypeStruct((8, HID), F32),
        ],
        in_specs=[any_spec] * 2 + [vmem_spec] * 2 + [any_spec, vmem_spec, vmem_spec, any_spec],
        out_specs=[vmem_spec] * 3,
        scratch_shapes=[
            vm((2, PLANE * PIECE, 128), F32),
            vm((PLANE * PIECE, 128), F32),
            vm((PLANE, PIECE, 128), F32),
            vm((PLANE, PIECE, 128), F32),
            vm((Z, OWN, 128), F32),
            vm((2, PLANE, PIECE, 128), F32),
            vm((PDIM, HID), BF16),
            vm((PDIM, HID), BF16),
            vm((PDIM, 2 * Q), BF16),
            vm((HID, 2 * Q), F32),
            vm((HID, 2 * Q), BF16),
            vm((PDIM, 2 * Q), F32),
            vm((2 * Z, PAIR, W), BF16),
            vm((2 * Z, Q, W), F32),
            vm((Q, PAIR), BF16),
            vm((2 * Z, Q, W), BF16),
            vm((Q, W), BF16),
            vm((Q, PAIR), F32),
            vm((Q, PAIR), F32),
            vm((Q, PAIR), F32),
            vm((2, 1, Q), F32),
            vm((2, CHIPS, 1, Q), F32),
            vm((PAIR, 128), F32),
            vm((2, Z, HALF, W), BF16),
            vm((2, Z, HALF, W), BF16),
            vm((2, 4, Q, W), BF16),
            vm((2, 4, Q, W), BF16),
            vm((1, Q), jnp.int32),
            vm((Q, PAIR), BF16),
            vm((Z, HALF, W), BF16),
            vm((Z, HALF, W), BF16),
            vm((2, 4, HALF, W), BF16),
            vm((2, 4, HALF, W), BF16),
            vm((2, 4, 2, HALF, W), BF16),
            vm((2, 4, 2, HALF, W), BF16),
            vm((HALF, W), BF16),
            vm((HALF, W), BF16),
            vm((Q, W), F32),
            dma((2 * Z + 3,)), dma((2 * Z,)), dma((2 * Z,)), dma((2,)),
            dma((2, CHIPS)), dma((2, CHIPS)),
            dma((2, Z)), dma((2, Z)), dma((2, 4)), dma((2, 4)), dma((2,)),
            dma((Z,)), dma((Z,)), dma((2, 4)), dma((2, 4)),
            dma((2, 4)), dma((2, 4)), dma((1,)), dma((1,)),
            dma((Z,)), dma((Z,)), dma((2, 4)), dma((2, 4)),
            dma((2, 4)), dma((2, 4)), dma((1,)), dma((1,)),
            dma((PLANE,)), dma((PLANE,)), dma((PLANE,)), dma((PLANE,)), dma((Z,)), dma((Z,)),
            dma((Z,)), dma((Z,)), dma((PLANE,)), dma((PLANE,)), dma((PLANE,)), dma((PLANE,)),
        ],
        compiler_params=pltpu.CompilerParams(
            collective_id=0, has_side_effects=True, vmem_limit_bytes=56 * 1024 * 1024),
        name="denoise_step",
    )(noise, refs, level, ids, w_in, bias, w_noise, w_outT)


def write_kernel(g_in_ref, g_outT_ref, small_ref, g_in_out, g_outT_out, bias_out, noise_out, loss_out):
    g_in_out[...] = g_in_ref[...]
    g_outT_out[...] = g_outT_ref[...]
    bias_out[...] = small_ref[0]
    noise_out[...] = small_ref[1]
    loss_out[...] = small_ref[2:3, 0:1] * (1.0 / FEATS)


def write_call(g_in, g_outT, small):
    vmem_spec = pl.BlockSpec(memory_space=pltpu.VMEM)
    shape = jax.ShapeDtypeStruct
    return pl.pallas_call(
        write_kernel,
        out_shape=[shape((PDIM, HID), F32)] * 2 + [shape((HID,), F32)] * 2 + [shape((1, 1), F32)],
        in_specs=[vmem_spec] * 3,
        out_specs=[vmem_spec] * 5,
        name="write_results",
    )(g_in, g_outT, small)


def per_device(noise_field, ref_crops, level_index, query_ids, w_in, bias_hidden, w_noise, w_out):
    g_in, g_outT, small = main_call(
        noise_field, ref_crops, level_index.reshape(1, Q), query_ids.reshape(1, Q), w_in,
        bias_hidden, w_noise, w_out.T)
    g_in, g_outT, bias, w_noise, loss = write_call(g_in, g_outT, small)
    return (g_in, g_outT.T, bias, w_noise, loss.reshape(()))


def solution(mesh):
    return jax.shard_map(
        per_device,
        mesh=mesh,
        in_specs=(P("query", None), P("ref", None), P("query"), P("query"), P(), P(), P(), P()),
        out_specs=(P(), P(), P(), P(), P()),
        check_vma=False,
    )
```

```python
import jax
import jax.numpy as jnp
from jax import lax
from jax.experimental import pallas as pl
from jax.experimental.pallas import tpu as pltpu
from jax.sharding import PartitionSpec as P

NLEV = 32
SIGMA_DATA = 0.5
MESH = pl.DeviceIdType.MESH
F32 = jnp.float32
BF16 = jnp.bfloat16

Z = 8
CHIPS = 2 * Z
Q = 256
HALF = 128
REF = 288
PAIR = 2 * REF
W = 384
PDIM = 192
HID = 768
NQ = 2048
FEATS = 12288
PLANE = 16
PP = 48
RP = 64
P_ROWS = PLANE * PP
ROWS = P_ROWS + Z * RP


def nt(a, b, **kw):
    return lax.dot_general(a, b, (((1,), (1,)), ((), ())), preferred_element_type=F32, **kw)


def tn(a, b, **kw):
    return lax.dot_general(a, b, (((0,), (0,)), ((), ())), preferred_element_type=F32, **kw)


def nn(a, b):
    return jnp.dot(a, b, preferred_element_type=F32)


def noise_level(index):
    low = 0.05 ** (1.0 / 7.0)
    high = 80.0 ** (1.0 / 7.0)
    frac = index.astype(F32) / (NLEV - 1)
    base = high + frac * (low - high)
    two = base * base
    return two * two * two * base


def column(row):
    return jnp.broadcast_to(row, (128, row.shape[1])).T[:, 0:1]


def row_of(col):
    return jnp.broadcast_to(col, (col.shape[0], 128)).T[0:8]


def main_kernel(
    noise_hbm, refs_hbm, level_ref, ids_ref, w_in_hbm, bias_ref, w_noise_ref, w_outT_hbm,
    g_in_ref, g_outT_ref, small_ref,
    grads, coreR, pS, pR, pzR, rS, rR, rxR, ryR, wholeP, wholeR,
    w_in_ref, w_outT_ref, scaled_ref, slope_ref, hidden_ref, fit_ref,
    refs, prod, match, noisy, noise, dots, halfS, halfR, statS, statR, sqacc,
    xS, xR, zS, zR2, idsR, match2,
    axS, axR, azS, azR, bzS, bzR, bxS, bxR, shareS,
    local_sem, swap_ss, swap_rs, half_sem, stat_ss, stat_rs,
    x_ss, x_rs, zz_ss, zz_rs, ids_sem,
    ax_ss, ax_rs, az_ss, az_rs, bz_ss, bz_rs, bx_ss, bx_rs,
    gax_ss, gax_rs, gaz_ss, gaz_rs, gbz_ss, gbz_rs, gbx_ss, gbx_rs,
    core_ss, core_rs, pp_ss, pp_rs, rz_ss, rz_rs, pz_ss, pz_rs, rx_ss, rx_rs, ry_ss, ry_rs,
    pshare_ss, pshare_rs, rshare_ss, rshare_rs, trade_ss, trade_rs,
):
    q = lax.axis_index("query")
    r = lax.axis_index("ref")
    core = r % 2
    chip = r // 2
    z = chip % Z
    xl = chip // Z
    other = 1 - xl

    def at(x_at, z_at, core_at):
        return (x_at * Z + z_at) * 2 + core_at

    x_hi = q // 4
    y = q % 4
    me = (x_hi * 2 + xl) * 4 + y

    def in_plane(p):
        return ((p // 8) * 4 + p % 4, at((p // 4) % 2, z, core))

    sib = at(xl, z, 1 - core)
    xn = at(other, z, core)
    to = (at(xl, (z + Z - 1) % Z, core), at(xl, (z + 1) % Z, core))

    def rcopy(src, dst, ssem, rsem, target):
        return pltpu.make_async_remote_copy(
            src_ref=src, dst_ref=dst, send_sem=ssem, recv_sem=rsem,
            device_id=(q, target), device_id_type=MESH)

    def order(i):
        d = 4 - (i + 1) // 2
        return (z + Z + d * (2 * (i % 2) - 1)) % Z

    def local_copy(b):
        off = pl.multiple_of(core * (FEATS // 2) + b * W, 128)
        return pltpu.make_async_copy(
            refs_hbm.at[:, pl.ds(off, W)], refs.at[b, pl.ds(core * REF, REF), :], local_sem.at[b])

    def swap_copy(b):
        off = pl.multiple_of((1 - core) * (FEATS // 2) + b * W, 128)
        return rcopy(
            refs_hbm.at[:, pl.ds(off, W)], refs.at[b, pl.ds(core * REF, REF), :],
            swap_ss.at[b], swap_rs.at[b], sib)

    def swap_landed(b):
        return rcopy(
            refs_hbm.at[:, pl.ds(0, W)], refs.at[b, pl.ds((1 - core) * REF, REF), :],
            swap_ss.at[b], swap_rs.at[b], sib)

    own = 2 * z + xl

    def start_local(i, _):
        o = order(i)
        local_copy(2 * o).start()
        local_copy(2 * o + 1).start()
        return 0

    lax.fori_loop(0, Z, start_local, 0)
    noise_off = pl.multiple_of(core * (FEATS // 2) + own * W, 128)
    noise_copy = pltpu.make_async_copy(
        noise_hbm.at[:, pl.ds(noise_off, W)], noise, local_sem.at[2 * Z])
    noise_copy.start()
    w_in_copy = pltpu.make_async_copy(w_in_hbm, w_in_ref, local_sem.at[2 * Z + 1])
    w_out_copy = pltpu.make_async_copy(w_outT_hbm, w_outT_ref, local_sem.at[2 * Z + 2])
    w_in_copy.start()
    w_out_copy.start()

    barrier = pltpu.get_barrier_semaphore()

    def greet(k, _):
        peer = (chip + k) % CHIPS
        pl.semaphore_signal(barrier, inc=1, device_id=(q, peer * 2 + core), device_id_type=MESH)
        return 0

    lax.fori_loop(1, CHIPS, greet, 0)
    pl.semaphore_signal(barrier, inc=1, device_id=(q, sib), device_id_type=MESH)

    def greet_plane(k, _):
        p = (me + k) % PLANE

        @pl.when(p != x_peer)
        def _():
            pl.semaphore_signal(barrier, inc=1, device_id=in_plane(p), device_id_type=MESH)

        return 0

    x_peer = (x_hi * 2 + other) * 4 + y
    lax.fori_loop(1, PLANE, greet_plane, 0)
    pl.semaphore_wait(barrier, CHIPS + PLANE - 2)

    sent = []

    def start_swap(i):
        o = order(i)
        swap_copy(2 * o).start()
        swap_copy(2 * o + 1).start()

    xo = at(other, z, core)
    q_xo = (1 - x_hi) * 4 + y
    ids_copy = pltpu.make_async_remote_copy(
        src_ref=ids_ref, dst_ref=idsR, send_sem=ids_sem.at[0], recv_sem=ids_sem.at[1],
        device_id=(q_xo, xo), device_id_type=MESH)
    ids_copy.start()
    sent.append(ids_copy.wait_send)
    for i in range(3):
        start_swap(i)

    def swap_sent():
        def one(b, _):
            swap_copy(b).wait_send()
            return 0

        lax.fori_loop(0, 2 * Z, one, 0)

    sent.append(swap_sent)

    sigma = noise_level(level_ref[...])
    sigma_col = column(sigma)
    places = lax.broadcasted_iota(jnp.int32, (Q, PAIR), 1).astype(F32)

    def one_hot(row):
        ids = column(row.astype(F32)) - (chip * PAIR).astype(F32)
        return (ids == places).astype(F32).astype(BF16)

    match[...] = one_hot(ids_ref[...])
    match2[0:HALF] = match[0:HALF]

    def x_copy(side, o):
        return pltpu.make_async_remote_copy(
            src_ref=xS.at[side, o], dst_ref=xR.at[side, o], send_sem=x_ss.at[side, o], recv_sem=x_rs.at[side, o],
            device_id=(q if side == 0 else q_xo, xn), device_id_type=MESH)

    def z_step(d, t):
        rows = pl.ds(HALF * d, HALF) if t == 0 else slice(None)
        return rcopy(zS.at[d, t, rows], zR2.at[d, t, rows], zz_ss.at[d, t], zz_rs.at[d, t], to[d])

    def first_multiply(i):
        o = order(i)
        if i + 3 < Z:
            start_swap(i + 3)
        for j in range(2):
            local_copy(2 * o + j).wait()
            swap_landed(2 * o + j).wait_recv()
        part = nn(match2[...], refs[2 * o + other]).astype(BF16)
        for side in range(2):
            xS[side, o] = part[side * HALF:(side + 1) * HALF]
            x_copy(side, o).start()
        prod[2 * o + xl] = nn(match[...], refs[2 * o + xl])

    def first_sum(o, side):
        x_copy(side, o).wait_recv()
        return prod[2 * o + xl, side * HALF:(side + 1) * HALF] + xR[side, o].astype(F32)

    def toward(d, t):
        return (z + Z + (2 * d - 1) * (4 - t)) % Z

    def first_reduce(idle):
        for i in range(3):
            first_multiply(i)
        for d in range(2):
            zS[d, 0, d * HALF:(d + 1) * HALF] = first_sum(toward(d, 0), d).astype(BF16)
            z_step(d, 0).start()
        for t in range(1, 4):
            for i in range(2 * t + 1, min(2 * t + 3, Z)):
                first_multiply(i)
            idle(t)
            for d in range(2):
                z_step(d, t - 1).wait_recv()
                for side in range(2):
                    rows = slice(side * HALF, (side + 1) * HALF)
                    part = first_sum(toward(d, t), side)
                    if t > 1 or side == d:
                        part = part + zR2[d, t - 1, rows].astype(F32)
                    zS[d, t, rows] = part.astype(BF16)
                z_step(d, t).start()
        idle(0)
        parts = [first_sum(z, side) for side in range(2)]
        for d in range(2):
            z_step(d, 3).wait_recv()
            for side in range(2):
                parts[side] = parts[side] + zR2[d, 3, side * HALF:(side + 1) * HALF].astype(F32)

        def finish():
            for d in range(2):
                for t in range(4):
                    z_step(d, t).wait_send()

            def one(o, _):
                x_copy(0, o).wait_send()
                x_copy(1, o).wait_send()
                return 0

            lax.fori_loop(0, Z, one, 0)

        sent.append(finish)
        return parts

    def reduce_scatter(idle):
        def ax(o):
            return rcopy(axS.at[o], axR.at[o], ax_ss.at[o], ax_rs.at[o], xn)

        def az(d, t):
            rows = pl.ds(64 * d, 64) if t == 0 else slice(None)
            return rcopy(azS.at[d, t, rows], azR.at[d, t, rows], az_ss.at[d, t], az_rs.at[d, t], to[d])

        def bz(d, t):
            if t == 0:
                return rcopy(bzS.at[d, 0, d], bzR.at[d, 0, d], bz_ss.at[d, 0], bz_rs.at[d, 0], to[d])
            return rcopy(bzS.at[d, t], bzR.at[d, t], bz_ss.at[d, t], bz_rs.at[d, t], to[d])

        def bx():
            return rcopy(bxS, bxR, bx_ss.at[0], bx_rs.at[0], xn)

        def multiply(i):
            o = order(i)
            for j in range(2):
                prod[2 * o + j] = nn(match[...], refs[2 * o + j])
            axS[o] = prod[2 * o + other, 0:HALF].astype(BF16)
            ax(o).start()

        multiply(0)
        for d in range(2):
            bzS[d, 0, d] = prod[2 * toward(d, 0) + d, HALF:Q].astype(BF16)
            bz(d, 0).start()
        multiply(1)
        multiply(2)
        idle(0)
        o = toward(0, 0)
        ax(o).wait_recv()
        for d in range(2):
            rows = slice(64 * d, 64 * d + 64)
            azS[d, 0, rows] = (prod[2 * o + xl, rows] + axR[o, rows].astype(F32)).astype(BF16)
            az(d, 0).start()
        for t in range(1, 4):
            for d in range(2):
                o = toward(d, t)
                bz(d, t - 1).wait_recv()
                for j in range(2):
                    s = prod[2 * o + j, HALF:Q]
                    if t > 1 or j == d:
                        s = s + bzR[d, t - 1, j].astype(F32)
                    bzS[d, t, j] = s.astype(BF16)
                bz(d, t).start()
            for i in range(2 * t + 1, min(2 * t + 3, Z)):
                multiply(i)
            for d in range(2):
                o = toward(d, t)
                ax(o).wait_recv()
                az(d, t - 1).wait_recv()
                s = prod[2 * o + xl, 0:HALF] + axR[o].astype(F32)
                if t > 1:
                    azS[d, t] = (s + azR[d, t - 1].astype(F32)).astype(BF16)
                else:
                    azS[d, t] = s.astype(BF16)
                    rows = slice(64 * d, 64 * d + 64)
                    azS[d, t, rows] = (s[rows] + azR[d, 0, rows].astype(F32)).astype(BF16)
                az(d, t).start()
            idle(t)
        for d in range(2):
            bz(d, 3).wait_recv()
        bxS[...] = (prod[2 * z + other, HALF:Q] + bzR[0, 3, other].astype(F32)
                    + bzR[1, 3, other].astype(F32)).astype(BF16)
        bx().start()
        ax(z).wait_recv()
        for d in range(2):
            az(d, 3).wait_recv()
        top = (prod[own, 0:HALF] + axR[z].astype(F32) + azR[0, 3].astype(F32) + azR[1, 3].astype(F32))
        bottom = prod[own, HALF:Q] + bzR[0, 3, xl].astype(F32) + bzR[1, 3, xl].astype(F32)
        bx().wait_recv()
        bottom = bottom + bxR[...].astype(F32)

        def finish():
            for d in range(2):
                for t in range(4):
                    az(d, t).wait_send()
                    bz(d, t).wait_send()
            bx().wait_send()

            def one(o, _):
                ax(o).wait_send()
                return 0

            lax.fori_loop(0, Z, one, 0)

        sent.append(finish)
        return top, bottom

    sqacc[...] = jnp.zeros_like(sqacc)

    def squares(t):
        def one(b, _):
            v = refs[b].astype(F32)
            v = v * v
            sqacc[...] += v[:, 0:128] + v[:, 128:256] + v[:, 256:384]
            return 0

        if t == 0:
            lax.fori_loop(0, 2 * Z, one, 0)

    ids_copy.wait_recv()
    match2[HALF:Q] = one_hot(idsR[...])[HALF:Q]
    top, bottom = first_reduce(squares)
    noise_copy.wait()
    noisy[own, 0:HALF] = (top + sigma_col[0:HALF] * noise[0:HALF].astype(F32)).astype(BF16)
    noisy[own, HALF:Q] = (bottom + sigma_col[HALF:Q] * noise[HALF:Q].astype(F32)).astype(BF16)

    def same(ref, ssem, rsem, target):
        return rcopy(ref, ref, ssem, rsem, target)

    def gax(o, x_at):
        return same(noisy.at[2 * o + x_at, 0:HALF], gax_ss.at[o], gax_rs.at[o], xn)

    def gbx(x_at):
        return same(noisy.at[2 * z + x_at, HALF:Q], gbx_ss.at[0], gbx_rs.at[0], xn)

    def gaz(d, s, o):
        if s == 4:
            view = noisy.at[2 * o + xl, pl.ds(64 * d, 64)]
        else:
            view = noisy.at[2 * o + xl, 0:HALF]
        return same(view, gaz_ss.at[d, s - 1], gaz_rs.at[d, s - 1], to[d])

    def gbz(d, s, o):
        if s == 4:
            view = noisy.at[2 * o + d, HALF:Q]
        else:
            view = noisy.at[pl.ds(2 * o, 2), HALF:Q]
        return same(view, gbz_ss.at[d, s - 1], gbz_rs.at[d, s - 1], to[d])

    def came(d, s):
        return (z + Z + (1 - 2 * d) * s) % Z

    def score(o, first=False):
        part = nt(noisy[2 * o], refs[2 * o]) + nt(noisy[2 * o + 1], refs[2 * o + 1])
        dots[...] = part if first else dots[...] + part

    gbx(xl).start()
    for d in range(2):
        gaz(d, 1, z).start()
    gax(z, xl).start()
    gbx(other).wait_recv()
    for d in range(2):
        gbz(d, 1, z).start()

    for s in range(1, 4):
        for d in range(2):
            o = came(d, s)
            gaz(d, s, o).wait_recv()
            gaz(d, s + 1, o).start()
            gax(o, xl).start()
        for d in range(2):
            o = came(d, s)
            gbz(d, s, o).wait_recv()
            gbz(d, s + 1, o).start()
        if s == 1:
            gax(z, other).wait_recv()
            score(z, True)
        else:
            for d in range(2):
                o = came(d, s - 1)
                gax(o, other).wait_recv()
                score(o)
    ref_sq = nt(jnp.ones((8, 128), F32), sqacc[...], precision=lax.Precision.HIGHEST)[0:1]
    o = came(0, 4)
    for d in range(2):
        gaz(d, 4, o).wait_recv()
    gax(o, xl).start()
    for d in range(2):
        gax(came(d, 3), other).wait_recv()
        score(came(d, 3))
    for d in range(2):
        gbz(d, 4, o).wait_recv()
    gax(o, other).wait_recv()
    score(o)

    def gather_sent():
        gbx(xl).wait_send()

        def one(o, _):
            gax(o, xl).wait_send()
            return 0

        lax.fori_loop(0, Z, one, 0)
        for d in range(2):
            for s in range(1, 5):
                gaz(d, s, z).wait_send()
                gbz(d, s, z).wait_send()

    sent.append(gather_sent)

    halfS[...] = 2.0 * dots[...] - ref_sq
    half = rcopy(halfS, halfR, half_sem.at[0], half_sem.at[1], sib)
    half.start()
    sent.append(half.wait_send)
    half.wait_recv()
    logits = (halfS[...] + halfR[...]) / (2.0 * sigma_col * sigma_col)
    dots[...] = logits

    def stat(i, k):
        peer = ((chip + k) % CHIPS) * 2 + core
        return rcopy(statS.at[i], statR.at[i, k], stat_ss.at[i, k], stat_rs.at[i, k], peer)

    def tell(i, col):
        statS[i] = row_of(col)[0:1]
        statR[i, 0] = statS[i]

        def one(k, _):
            stat(i, k).start()
            return 0

        lax.fori_loop(1, CHIPS, one, 0)

        def told():
            def one(k, _):
                stat(i, k).wait_send()
                return 0

            lax.fori_loop(1, CHIPS, one, 0)

        sent.append(told)

    def hear(i):
        def one(k, _):
            stat(i, k).wait_recv()
            return 0

        lax.fori_loop(1, CHIPS, one, 0)

    mine = jnp.max(logits, axis=1, keepdims=True)
    tell(0, mine)
    dots[...] = jnp.exp(logits - mine)
    hear(0)
    peak = column(jnp.max(statR[0], axis=0))
    match[...] = (dots[...] * jnp.exp(mine - peak)).astype(BF16)

    def patches(t):
        return jnp.concatenate([t[0:PDIM], t[PDIM:W]], axis=1)

    def twice(t):
        return jnp.concatenate([t, t], axis=1)

    s = twice(sigma)
    var = s * s + SIGMA_DATA * SIGMA_DATA
    c_skip = SIGMA_DATA * SIGMA_DATA / var
    c_out = s * SIGMA_DATA / jnp.sqrt(var)
    c_in = 1.0 / jnp.sqrt(var)
    c_noise = jnp.log(s) / 4.0

    def forward(t):
        if t == 0:
            tell(1, jnp.sum(match[...].astype(F32), axis=1, keepdims=True))
            w_in_copy.wait()
            w_out_copy.wait()
        elif t == 1:
            x_full = patches(noisy[own].astype(F32).T)
            scaled = (c_in * x_full).astype(BF16)
            scaled_ref[...] = scaled
            fit_ref[...] = c_skip * x_full / c_out
            slope_ref[...] = (tn(w_in_ref[...], scaled) + column(w_noise_ref[...].reshape(1, HID)) * c_noise
                              + column(bias_ref[...].reshape(1, HID)))
        elif t == 2:
            pre = slope_ref[...]
            sig_p = jax.nn.sigmoid(pre)
            hidden_ref[...] = (pre * sig_p).astype(BF16)
            slope_ref[...] = sig_p * (1.0 + pre * (1.0 - sig_p))
        else:
            fit_ref[...] += nn(w_outT_ref[...], hidden_ref[...])

    top, bottom = reduce_scatter(forward)
    shareS[0:HALF] = top
    shareS[HALF:Q] = bottom
    hear(1)
    total = jnp.sum(statR[1], axis=0)

    resid = fit_ref[...] - patches(shareS[...].T / total) / c_out
    g_b = (2.0 / NQ * resid).astype(BF16)

    def strips(at_row, value):
        rows = value.shape[0]
        for h in range(2):
            for k in range(3):
                cols = slice(h * W + k * 128, h * W + k * 128 + 128)
                grads[h, at_row + k * rows:at_row + (k + 1) * rows] = value[:, cols]

    def core_copy(i):
        rows = (pl.ds(0, P_ROWS), pl.ds(P_ROWS, Z * RP))[i]
        return rcopy(grads.at[1 - core, rows], coreR.at[rows], core_ss.at[i], core_rs.at[i], sib)

    def loop(first, last, body):
        def one(k, _):
            body(k)
            return 0

        lax.fori_loop(first, last, one, 0)

    def plane_copy(src, dst, ssem, rsem, p):
        return pltpu.make_async_remote_copy(
            src_ref=src, dst_ref=dst, send_sem=ssem, recv_sem=rsem, device_id=in_plane(p), device_id_type=MESH)

    def z_copy(src, dst, ssem, rsem, o):
        return rcopy(src, dst, ssem, rsem, at(xl, o, core))

    x = me // 4

    def pp(k):
        p = (me + k) % PLANE
        return plane_copy(pS.at[p], pR.at[k], pp_ss.at[k], pp_rs.at[k], p)

    def rz(k):
        o = (z + k) % Z
        return z_copy(rS.at[o], rR.at[k], rz_ss.at[k], rz_rs.at[k], o)

    def pz(k, origin):
        view = pzR.at[origin]
        return z_copy(view, view, pz_ss.at[k], pz_rs.at[origin], (z + k) % Z)

    def rx(k, origin):
        view = rxR.at[origin]
        return plane_copy(view, view, rx_ss.at[k], rx_rs.at[origin], ((x + k) % 4) * 4 + y)

    def ry(k, origin):
        view = ryR.at[origin]
        return plane_copy(view, view, ry_ss.at[k], ry_rs.at[origin], x * 4 + (y + k) % 4)

    def pshare(k, p):
        view = wholeP.at[core, p]
        return plane_copy(view, view, pshare_ss.at[k], pshare_rs.at[p], (me + k) % PLANE)

    def rshare(k, o):
        view = wholeR.at[core, o]
        return z_copy(view, view, rshare_ss.at[k], rshare_rs.at[o], (z + k) % Z)

    def ptrade(h, p):
        return rcopy(wholeP.at[h, p], wholeP.at[h, p], trade_ss.at[p], trade_rs.at[p], sib)

    def rtrade(h, o):
        return rcopy(wholeR.at[h, o], wholeR.at[h, o], trade_ss.at[PLANE + o], trade_rs.at[PLANE + o], sib)

    strips(0, nt(g_b, hidden_ref[...]))
    dpre = tn(w_outT_ref[...], g_b) * slope_ref[...]
    strips(3 * PDIM, nt(scaled_ref[...], dpre.astype(BF16)))
    core_copy(0).start()
    objective = jnp.sum(resid * resid) / NQ
    rows = lax.broadcasted_iota(jnp.int32, (8, 2 * Q), 0)
    pick = jnp.where(rows == 0, 1.0, jnp.where(rows == 1, c_noise, 0.0))
    small = nt(pick, dpre, precision=lax.Precision.HIGHEST)
    strips(6 * PDIM, jnp.where(lax.broadcasted_iota(jnp.int32, (8, HID), 0) == 2, objective, small))
    for h in range(2):
        grads[h, 6 * PDIM + 24:] = jnp.zeros((ROWS - 6 * PDIM - 24, 128), F32)
    core_copy(1).start()
    core_copy(0).wait_recv()
    pS[...] = (grads[core, 0:P_ROWS] + coreR[0:P_ROWS]).reshape(PLANE, PP, 128)
    loop(1, PLANE, lambda k: pp(k).start())
    core_copy(1).wait_recv()
    rS[...] = (grads[core, P_ROWS:] + coreR[P_ROWS:]).reshape(Z, RP, 128)
    loop(1, Z, lambda k: rz(k).start())

    pR[0] = pS[me]

    def add_pp(k):
        pp(k).wait_recv()
        pR[0] += pR[k]

    loop(1, PLANE, add_pp)
    pzR[z] = pR[0]
    loop(1, Z, lambda k: pz(k, z).start())
    rR[0] = rS[z]

    def add_rz(k):
        rz(k).wait_recv()
        rR[0] += rR[k]

    loop(1, Z, add_rz)
    rxR[x] = rR[0]
    loop(1, 4, lambda k: rx(k, x).start())
    loop(1, 4, lambda k: rx(k, (x + k) % 4).wait_recv())
    ryR[y] = jnp.sum(rxR[...], axis=0)
    loop(1, 4, lambda k: ry(k, y).start())
    loop(1, Z, lambda k: pz(k, (z + k) % Z).wait_recv())
    wholeP[core, me] = jnp.sum(pzR[...], axis=0)
    loop(1, PLANE, lambda k: pshare(k, me).start())
    loop(1, 4, lambda k: ry(k, (y + k) % 4).wait_recv())
    wholeR[core, z] = jnp.sum(ryR[...], axis=0)
    loop(1, Z, lambda k: rshare(k, z).start())
    ptrade(core, me).start()
    rtrade(core, z).start()

    def pass_r(k):
        o = (z + Z - k) % Z
        rshare(k, o).wait_recv()
        rtrade(core, o).start()

    def pass_p(k):
        p = (me + PLANE - k) % PLANE
        pshare(k, p).wait_recv()
        ptrade(core, p).start()

    loop(1, Z, pass_r)
    loop(1, PLANE, pass_p)
    loop(0, Z, lambda o: rtrade(1 - core, o).wait_recv())
    loop(0, PLANE, lambda p: ptrade(1 - core, p).wait_recv())
    for h in range(2):
        first = wholeP[h].reshape(P_ROWS, 128)
        second = wholeR[h].reshape(Z * RP, 128)
        for k in range(3):
            cols = slice(h * W + k * 128, h * W + k * 128 + 128)
            g_outT_ref[:, cols] = first[k * PDIM:(k + 1) * PDIM]
            g_in_ref[:, cols] = first[3 * PDIM:] if k == 0 else second[(k - 1) * PDIM:k * PDIM]
            small_ref[:, cols] = second[2 * PDIM + 8 * k:2 * PDIM + 8 * k + 8]

    for i in range(2):
        core_copy(i).wait_send()
    loop(0, PLANE, lambda p: ptrade(core, p).wait_send())
    loop(0, Z, lambda o: rtrade(core, o).wait_send())

    def plane_sent(k):
        pp(k).wait_send()
        pshare(k, me).wait_send()

    def z_sent(k):
        rz(k).wait_send()
        pz(k, z).wait_send()
        rshare(k, z).wait_send()

    def side_sent(k):
        rx(k, x).wait_send()
        ry(k, y).wait_send()

    loop(1, PLANE, plane_sent)
    loop(1, Z, z_sent)
    loop(1, 4, side_sent)
    for wait in sent:
        wait()


def main_call(noise, refs, level, ids, w_in, bias, w_noise, w_outT):
    dma = pltpu.SemaphoreType.DMA
    vm = pltpu.VMEM
    any_spec = pl.BlockSpec(memory_space=pl.ANY)
    vmem_spec = pl.BlockSpec(memory_space=pltpu.VMEM)
    return pl.pallas_call(
        main_kernel,
        out_shape=[
            jax.ShapeDtypeStruct((PDIM, HID), F32),
            jax.ShapeDtypeStruct((PDIM, HID), F32),
            jax.ShapeDtypeStruct((8, HID), F32),
        ],
        in_specs=[any_spec] * 2 + [vmem_spec] * 2 + [any_spec, vmem_spec, vmem_spec, any_spec],
        out_specs=[vmem_spec] * 3,
        scratch_shapes=[
            vm((2, ROWS, 128), F32),
            vm((ROWS, 128), F32),
            vm((PLANE, PP, 128), F32),
            vm((PLANE, PP, 128), F32),
            vm((Z, PP, 128), F32),
            vm((Z, RP, 128), F32),
            vm((Z, RP, 128), F32),
            vm((4, RP, 128), F32),
            vm((4, RP, 128), F32),
            vm((2, PLANE, PP, 128), F32),
            vm((2, Z, RP, 128), F32),
            vm((PDIM, HID), BF16),
            vm((PDIM, HID), BF16),
            vm((PDIM, 2 * Q), BF16),
            vm((HID, 2 * Q), F32),
            vm((HID, 2 * Q), BF16),
            vm((PDIM, 2 * Q), F32),
            vm((2 * Z, PAIR, W), BF16),
            vm((2 * Z, Q, W), F32),
            vm((Q, PAIR), BF16),
            vm((2 * Z, Q, W), BF16),
            vm((Q, W), BF16),
            vm((Q, PAIR), F32),
            vm((Q, PAIR), F32),
            vm((Q, PAIR), F32),
            vm((2, 1, Q), F32),
            vm((2, CHIPS, 1, Q), F32),
            vm((PAIR, 128), F32),
            vm((2, Z, HALF, W), BF16),
            vm((2, Z, HALF, W), BF16),
            vm((2, 4, Q, W), BF16),
            vm((2, 4, Q, W), BF16),
            vm((1, Q), jnp.int32),
            vm((Q, PAIR), BF16),
            vm((Z, HALF, W), BF16),
            vm((Z, HALF, W), BF16),
            vm((2, 4, HALF, W), BF16),
            vm((2, 4, HALF, W), BF16),
            vm((2, 4, 2, HALF, W), BF16),
            vm((2, 4, 2, HALF, W), BF16),
            vm((HALF, W), BF16),
            vm((HALF, W), BF16),
            vm((Q, W), F32),
            dma((2 * Z + 3,)), dma((2 * Z,)), dma((2 * Z,)), dma((2,)),
            dma((2, CHIPS)), dma((2, CHIPS)),
            dma((2, Z)), dma((2, Z)), dma((2, 4)), dma((2, 4)), dma((2,)),
            dma((Z,)), dma((Z,)), dma((2, 4)), dma((2, 4)),
            dma((2, 4)), dma((2, 4)), dma((1,)), dma((1,)),
            dma((Z,)), dma((Z,)), dma((2, 4)), dma((2, 4)),
            dma((2, 4)), dma((2, 4)), dma((1,)), dma((1,)),
            dma((2,)), dma((2,)), dma((PLANE,)), dma((PLANE,)), dma((Z,)), dma((Z,)),
            dma((Z,)), dma((Z,)), dma((4,)), dma((4,)), dma((4,)), dma((4,)),
            dma((PLANE,)), dma((PLANE,)), dma((Z,)), dma((Z,)), dma((PLANE + Z,)), dma((PLANE + Z,)),
        ],
        compiler_params=pltpu.CompilerParams(
            collective_id=0, has_side_effects=True, vmem_limit_bytes=56 * 1024 * 1024),
        name="denoise_step",
    )(noise, refs, level, ids, w_in, bias, w_noise, w_outT)


def write_kernel(g_in_ref, g_outT_ref, small_ref, g_in_out, g_outT_out, bias_out, noise_out, loss_out):
    g_in_out[...] = g_in_ref[...]
    g_outT_out[...] = g_outT_ref[...]
    bias_out[...] = small_ref[0]
    noise_out[...] = small_ref[1]
    loss_out[...] = small_ref[2:3, 0:1] * (1.0 / FEATS)


def write_call(g_in, g_outT, small):
    vmem_spec = pl.BlockSpec(memory_space=pltpu.VMEM)
    shape = jax.ShapeDtypeStruct
    return pl.pallas_call(
        write_kernel,
        out_shape=[shape((PDIM, HID), F32)] * 2 + [shape((HID,), F32)] * 2 + [shape((1, 1), F32)],
        in_specs=[vmem_spec] * 3,
        out_specs=[vmem_spec] * 5,
        name="write_results",
    )(g_in, g_outT, small)


def per_device(noise_field, ref_crops, level_index, query_ids, w_in, bias_hidden, w_noise, w_out):
    g_in, g_outT, small = main_call(
        noise_field, ref_crops, level_index.reshape(1, Q), query_ids.reshape(1, Q), w_in,
        bias_hidden, w_noise, w_out.T)
    g_in, g_outT, bias, w_noise, loss = write_call(g_in, g_outT, small)
    return (g_in, g_outT.T, bias, w_noise, loss.reshape(()))


def solution(mesh):
    return jax.shard_map(
        per_device,
        mesh=mesh,
        in_specs=(P("query", None), P("ref", None), P("query"), P("query"), P(), P(), P(), P()),
        out_specs=(P(), P(), P(), P(), P()),
        check_vma=False,
    )
```

```python
import jax
import jax.numpy as jnp
from jax import lax
from jax.experimental import pallas as pl
from jax.experimental.pallas import tpu as pltpu
from jax.sharding import PartitionSpec as P

NLEV = 32
SIGMA_DATA = 0.5
MESH = pl.DeviceIdType.MESH
F32 = jnp.float32
BF16 = jnp.bfloat16

Z = 8
CHIPS = 2 * Z
Q = 256
HALF = 128
NA = 160
NB = Q - NA
NA0 = 80
REF = 288
PAIR = 2 * REF
W = 384
PDIM = 192
HID = 768
NQ = 2048
FEATS = 12288
PLANE = 16
PP = 48
RP = 64
P_ROWS = PLANE * PP
ROWS = P_ROWS + Z * RP


def nt(a, b, **kw):
    return lax.dot_general(a, b, (((1,), (1,)), ((), ())), preferred_element_type=F32, **kw)


def tn(a, b, **kw):
    return lax.dot_general(a, b, (((0,), (0,)), ((), ())), preferred_element_type=F32, **kw)


def nn(a, b):
    return jnp.dot(a, b, preferred_element_type=F32)


def noise_level(index):
    low = 0.05 ** (1.0 / 7.0)
    high = 80.0 ** (1.0 / 7.0)
    frac = index.astype(F32) / (NLEV - 1)
    base = high + frac * (low - high)
    two = base * base
    return two * two * two * base


def column(row):
    return jnp.broadcast_to(row, (128, row.shape[1])).T[:, 0:1]


def row_of(col):
    return jnp.broadcast_to(col, (col.shape[0], 128)).T[0:8]


def main_kernel(
    noise_hbm, refs_hbm, level_ref, ids_ref, w_in_hbm, bias_ref, w_noise_ref, w_outT_hbm,
    g_in_ref, g_outT_ref, small_ref,
    grads, coreR, pS, pR, pzR, rS, rR, rxR, ryR, wholeP, wholeR,
    w_in_ref, w_outT_ref, scaled_ref, slope_ref, hidden_ref, fit_ref,
    refs, prod, match, noisy, noise, dots, halfS, halfR, statS, statR, sqacc,
    xS, xR, zS, zR2, idsR, match2,
    axS, axR, azS, azR, bzS, bzR, bxS, bxR, shareS,
    local_sem, swap_ss, swap_rs, half_sem, stat_ss, stat_rs,
    x_ss, x_rs, zz_ss, zz_rs, ids_sem,
    ax_ss, ax_rs, az_ss, az_rs, bz_ss, bz_rs, bx_ss, bx_rs,
    gax_ss, gax_rs, gaz_ss, gaz_rs, gbz_ss, gbz_rs, gbx_ss, gbx_rs,
    core_ss, core_rs, pp_ss, pp_rs, rz_ss, rz_rs, pz_ss, pz_rs, rx_ss, rx_rs, ry_ss, ry_rs,
    pshare_ss, pshare_rs, rshare_ss, rshare_rs, trade_ss, trade_rs,
):
    q = lax.axis_index("query")
    r = lax.axis_index("ref")
    core = r % 2
    chip = r // 2
    z = chip % Z
    xl = chip // Z
    other = 1 - xl

    def at(x_at, z_at, core_at):
        return (x_at * Z + z_at) * 2 + core_at

    x_hi = q // 4
    y = q % 4
    me = (x_hi * 2 + xl) * 4 + y

    def in_plane(p):
        return ((p // 8) * 4 + p % 4, at((p // 4) % 2, z, core))

    sib = at(xl, z, 1 - core)
    xn = at(other, z, core)
    to = (at(xl, (z + Z - 1) % Z, core), at(xl, (z + 1) % Z, core))

    def rcopy(src, dst, ssem, rsem, target):
        return pltpu.make_async_remote_copy(
            src_ref=src, dst_ref=dst, send_sem=ssem, recv_sem=rsem,
            device_id=(q, target), device_id_type=MESH)

    def order(i):
        d = 4 - (i + 1) // 2
        return (z + Z + d * (2 * (i % 2) - 1)) % Z

    def local_copy(b):
        off = pl.multiple_of(core * (FEATS // 2) + b * W, 128)
        return pltpu.make_async_copy(
            refs_hbm.at[:, pl.ds(off, W)], refs.at[b, pl.ds(core * REF, REF), :], local_sem.at[b])

    def swap_copy(b):
        off = pl.multiple_of((1 - core) * (FEATS // 2) + b * W, 128)
        return rcopy(
            refs_hbm.at[:, pl.ds(off, W)], refs.at[b, pl.ds(core * REF, REF), :],
            swap_ss.at[b], swap_rs.at[b], sib)

    def swap_landed(b):
        return rcopy(
            refs_hbm.at[:, pl.ds(0, W)], refs.at[b, pl.ds((1 - core) * REF, REF), :],
            swap_ss.at[b], swap_rs.at[b], sib)

    own = 2 * z + xl

    def start_local(i, _):
        o = order(i)
        local_copy(2 * o).start()
        local_copy(2 * o + 1).start()
        return 0

    lax.fori_loop(0, Z, start_local, 0)
    noise_off = pl.multiple_of(core * (FEATS // 2) + own * W, 128)
    noise_copy = pltpu.make_async_copy(
        noise_hbm.at[:, pl.ds(noise_off, W)], noise, local_sem.at[2 * Z])
    noise_copy.start()
    w_in_copy = pltpu.make_async_copy(w_in_hbm, w_in_ref, local_sem.at[2 * Z + 1])
    w_out_copy = pltpu.make_async_copy(w_outT_hbm, w_outT_ref, local_sem.at[2 * Z + 2])
    w_in_copy.start()
    w_out_copy.start()

    barrier = pltpu.get_barrier_semaphore()

    def greet(k, _):
        peer = (chip + k) % CHIPS
        pl.semaphore_signal(barrier, inc=1, device_id=(q, peer * 2 + core), device_id_type=MESH)
        return 0

    lax.fori_loop(1, CHIPS, greet, 0)
    pl.semaphore_signal(barrier, inc=1, device_id=(q, sib), device_id_type=MESH)

    def greet_plane(k, _):
        p = (me + k) % PLANE

        @pl.when(p != x_peer)
        def _():
            pl.semaphore_signal(barrier, inc=1, device_id=in_plane(p), device_id_type=MESH)

        return 0

    x_peer = (x_hi * 2 + other) * 4 + y
    lax.fori_loop(1, PLANE, greet_plane, 0)
    pl.semaphore_wait(barrier, CHIPS + PLANE - 2)

    sent = []

    def start_swap(i):
        o = order(i)
        swap_copy(2 * o).start()
        swap_copy(2 * o + 1).start()

    xo = at(other, z, core)
    q_xo = (1 - x_hi) * 4 + y
    ids_copy = pltpu.make_async_remote_copy(
        src_ref=ids_ref, dst_ref=idsR, send_sem=ids_sem.at[0], recv_sem=ids_sem.at[1],
        device_id=(q_xo, xo), device_id_type=MESH)
    ids_copy.start()
    sent.append(ids_copy.wait_send)
    for i in range(3):
        start_swap(i)

    def swap_sent():
        def one(b, _):
            swap_copy(b).wait_send()
            return 0

        lax.fori_loop(0, 2 * Z, one, 0)

    sent.append(swap_sent)

    sigma = noise_level(level_ref[...])
    sigma_col = column(sigma)
    places = lax.broadcasted_iota(jnp.int32, (Q, PAIR), 1).astype(F32)

    def one_hot(row):
        ids = column(row.astype(F32)) - (chip * PAIR).astype(F32)
        return (ids == places).astype(F32).astype(BF16)

    match[...] = one_hot(ids_ref[...])
    match2[0:HALF] = match[0:HALF]

    def x_copy(side, o):
        return pltpu.make_async_remote_copy(
            src_ref=xS.at[side, o], dst_ref=xR.at[side, o], send_sem=x_ss.at[side, o], recv_sem=x_rs.at[side, o],
            device_id=(q if side == 0 else q_xo, xn), device_id_type=MESH)

    def z_step(d, t, side):
        rows = pl.ds(HALF * side, HALF)
        return rcopy(zS.at[d, t, rows], zR2.at[d, t, rows], zz_ss.at[d, t, side], zz_rs.at[d, t, side], to[d])

    def first_multiply(i):
        o = order(i)
        if i + 3 < Z:
            start_swap(i + 3)
        for j in range(2):
            local_copy(2 * o + j).wait()
            swap_landed(2 * o + j).wait_recv()
        part = nn(match2[...], refs[2 * o + other]).astype(BF16)
        for side in range(2):
            xS[side, o] = part[side * HALF:(side + 1) * HALF]
            x_copy(side, o).start()
        prod[2 * o + xl] = nn(match[...], refs[2 * o + xl])

    def first_sum(o, side):
        x_copy(side, o).wait_recv()
        return prod[2 * o + xl, side * HALF:(side + 1) * HALF] + xR[side, o].astype(F32)

    def toward(d, t):
        return (z + Z + (2 * d - 1) * (4 - t)) % Z

    def opposite(d):
        return pl.ds(NA0 * d, (NA0, NA - NA0)[d])

    def first_reduce(idle):
        for i in range(3):
            first_multiply(i)
        for d in range(2):
            zS[d, 0, d * HALF:(d + 1) * HALF] = first_sum(toward(d, 0), d).astype(BF16)
            z_step(d, 0, d).start()
        for t in range(1, 4):
            for i in range(2 * t + 1, min(2 * t + 3, Z)):
                first_multiply(i)
            idle(t)
            for side in range(2):
                rows = slice(side * HALF, (side + 1) * HALF)
                for d in range(2):
                    part = first_sum(toward(d, t), side)
                    if t > 1 or side == d:
                        z_step(d, t - 1, side).wait_recv()
                        part = part + zR2[d, t - 1, rows].astype(F32)
                    zS[d, t, rows] = part.astype(BF16)
                    z_step(d, t, side).start()
        idle(0)
        parts = [first_sum(z, side) for side in range(2)]
        for side in range(2):
            for d in range(2):
                z_step(d, 3, side).wait_recv()
                parts[side] = parts[side] + zR2[d, 3, side * HALF:(side + 1) * HALF].astype(F32)

        def finish():
            for d in range(2):
                z_step(d, 0, d).wait_send()
                for t in range(1, 4):
                    for side in range(2):
                        z_step(d, t, side).wait_send()

            def one(o, _):
                x_copy(0, o).wait_send()
                x_copy(1, o).wait_send()
                return 0

            lax.fori_loop(0, Z, one, 0)

        sent.append(finish)
        return parts

    def reduce_scatter(idle):
        def ax(o):
            return rcopy(axS.at[o], axR.at[o], ax_ss.at[o], ax_rs.at[o], xn)

        def az(d, t):
            rows = opposite(d) if t == 0 else slice(None)
            return rcopy(azS.at[d, t, rows], azR.at[d, t, rows], az_ss.at[d, t], az_rs.at[d, t], to[d])

        def bz(d, t, j):
            return rcopy(bzS.at[d, t, j], bzR.at[d, t, j], bz_ss.at[d, t, j], bz_rs.at[d, t, j], to[d])

        def bx():
            return rcopy(bxS, bxR, bx_ss.at[0], bx_rs.at[0], xn)

        def multiply(i):
            o = order(i)
            for j in range(2):
                prod[2 * o + j] = nn(match[...], refs[2 * o + j])
            axS[o] = prod[2 * o + other, 0:NA].astype(BF16)
            ax(o).start()

        multiply(0)
        for d in range(2):
            bzS[d, 0, d] = prod[2 * toward(d, 0) + d, NA:Q].astype(BF16)
            bz(d, 0, d).start()
        multiply(1)
        multiply(2)
        idle(0)
        o = toward(0, 0)
        ax(o).wait_recv()
        for d in range(2):
            rows = opposite(d)
            azS[d, 0, rows] = (prod[2 * o + xl, rows] + axR[o, rows].astype(F32)).astype(BF16)
            az(d, 0).start()
        for t in range(1, 4):
            for j in range(2):
                for d in range(2):
                    s = prod[2 * toward(d, t) + j, NA:Q]
                    if t > 1 or j == d:
                        bz(d, t - 1, j).wait_recv()
                        s = s + bzR[d, t - 1, j].astype(F32)
                    bzS[d, t, j] = s.astype(BF16)
                    bz(d, t, j).start()
            for i in range(2 * t + 1, min(2 * t + 3, Z)):
                multiply(i)
            for d in range(2):
                o = toward(d, t)
                ax(o).wait_recv()
                az(d, t - 1).wait_recv()
                s = prod[2 * o + xl, 0:NA] + axR[o].astype(F32)
                if t > 1:
                    azS[d, t] = (s + azR[d, t - 1].astype(F32)).astype(BF16)
                else:
                    azS[d, t] = s.astype(BF16)
                    rows = opposite(d)
                    azS[d, t, rows] = (s[rows.start:rows.start + rows.size] + azR[d, 0, rows].astype(F32)).astype(BF16)
                az(d, t).start()
            idle(t)
        for d in range(2):
            for j in range(2):
                bz(d, 3, j).wait_recv()
        bxS[...] = (prod[2 * z + other, NA:Q] + bzR[0, 3, other].astype(F32)
                    + bzR[1, 3, other].astype(F32)).astype(BF16)
        bx().start()
        ax(z).wait_recv()
        for d in range(2):
            az(d, 3).wait_recv()
        top = (prod[own, 0:NA] + axR[z].astype(F32) + azR[0, 3].astype(F32) + azR[1, 3].astype(F32))
        bottom = prod[own, NA:Q] + bzR[0, 3, xl].astype(F32) + bzR[1, 3, xl].astype(F32)
        bx().wait_recv()
        bottom = bottom + bxR[...].astype(F32)

        def finish():
            for d in range(2):
                bz(d, 0, d).wait_send()
                for t in range(4):
                    az(d, t).wait_send()
                for t in range(1, 4):
                    for j in range(2):
                        bz(d, t, j).wait_send()
            bx().wait_send()

            def one(o, _):
                ax(o).wait_send()
                return 0

            lax.fori_loop(0, Z, one, 0)

        sent.append(finish)
        return top, bottom

    sqacc[...] = jnp.zeros_like(sqacc)

    def squares(t):
        def one(b, _):
            v = refs[b].astype(F32)
            v = v * v
            sqacc[...] += v[:, 0:128] + v[:, 128:256] + v[:, 256:384]
            return 0

        if t == 0:
            lax.fori_loop(0, 2 * Z, one, 0)

    ids_copy.wait_recv()
    match2[HALF:Q] = one_hot(idsR[...])[HALF:Q]
    top, bottom = first_reduce(squares)
    noise_copy.wait()
    noisy[own, 0:HALF] = (top + sigma_col[0:HALF] * noise[0:HALF].astype(F32)).astype(BF16)
    noisy[own, HALF:Q] = (bottom + sigma_col[HALF:Q] * noise[HALF:Q].astype(F32)).astype(BF16)

    def same(ref, ssem, rsem, target):
        return rcopy(ref, ref, ssem, rsem, target)

    def gax(o, x_at):
        return same(noisy.at[2 * o + x_at, 0:NA], gax_ss.at[o], gax_rs.at[o], xn)

    def gbx(x_at):
        return same(noisy.at[2 * z + x_at, NA:Q], gbx_ss.at[0], gbx_rs.at[0], xn)

    def gaz(d, s, o):
        if s == 4:
            view = noisy.at[2 * o + xl, opposite(d)]
        else:
            view = noisy.at[2 * o + xl, 0:NA]
        return same(view, gaz_ss.at[d, s - 1], gaz_rs.at[d, s - 1], to[d])

    def gbz(d, s, o, j):
        return same(noisy.at[2 * o + j, NA:Q], gbz_ss.at[d, s - 1, j], gbz_rs.at[d, s - 1, j], to[d])

    def came(d, s):
        return (z + Z + (1 - 2 * d) * s) % Z

    def score(o, first=False):
        part = nt(noisy[2 * o], refs[2 * o]) + nt(noisy[2 * o + 1], refs[2 * o + 1])
        dots[...] = part if first else dots[...] + part

    gbx(xl).start()
    for d in range(2):
        gaz(d, 1, z).start()
    for d in range(2):
        gbz(d, 1, z, xl).start()
    gax(z, xl).start()
    gbx(other).wait_recv()
    for d in range(2):
        gbz(d, 1, z, other).start()

    for s in range(1, 4):
        for d in range(2):
            o = came(d, s)
            gaz(d, s, o).wait_recv()
            gaz(d, s + 1, o).start()
            gax(o, xl).start()
        for j in (xl, other) if s < 3 else (0, 1):
            for d in range(2):
                o = came(d, s)
                gbz(d, s, o, j).wait_recv()
                if s < 3 or j == d:
                    gbz(d, s + 1, o, j).start()
        if s == 1:
            gax(z, other).wait_recv()
            score(z, True)
        else:
            for d in range(2):
                o = came(d, s - 1)
                gax(o, other).wait_recv()
                score(o)
    ref_sq = nt(jnp.ones((8, 128), F32), sqacc[...], precision=lax.Precision.HIGHEST)[0:1]
    o = came(0, 4)
    for d in range(2):
        gaz(d, 4, o).wait_recv()
    gax(o, xl).start()
    for d in range(2):
        gax(came(d, 3), other).wait_recv()
        score(came(d, 3))
    for d in range(2):
        gbz(d, 4, o, d).wait_recv()
    gax(o, other).wait_recv()
    score(o)

    def gather_sent():
        gbx(xl).wait_send()

        def one(o, _):
            gax(o, xl).wait_send()
            return 0

        lax.fori_loop(0, Z, one, 0)
        for d in range(2):
            for s in range(1, 5):
                gaz(d, s, z).wait_send()
                for j in range(2):
                    if s < 4 or j == d:
                        gbz(d, s, z, j).wait_send()

    sent.append(gather_sent)

    halfS[...] = 2.0 * dots[...] - ref_sq
    half = rcopy(halfS, halfR, half_sem.at[0], half_sem.at[1], sib)
    half.start()
    sent.append(half.wait_send)
    half.wait_recv()
    logits = (halfS[...] + halfR[...]) / (2.0 * sigma_col * sigma_col)
    dots[...] = logits

    def stat(i, k):
        peer = ((chip + k) % CHIPS) * 2 + core
        return rcopy(statS.at[i], statR.at[i, k], stat_ss.at[i, k], stat_rs.at[i, k], peer)

    def tell(i, col):
        statS[i] = row_of(col)[0:1]
        statR[i, 0] = statS[i]

        def one(k, _):
            stat(i, k).start()
            return 0

        lax.fori_loop(1, CHIPS, one, 0)

        def told():
            def one(k, _):
                stat(i, k).wait_send()
                return 0

            lax.fori_loop(1, CHIPS, one, 0)

        sent.append(told)

    def hear(i):
        def one(k, _):
            stat(i, k).wait_recv()
            return 0

        lax.fori_loop(1, CHIPS, one, 0)

    mine = jnp.max(logits, axis=1, keepdims=True)
    tell(0, mine)
    dots[...] = jnp.exp(logits - mine)
    hear(0)
    peak = column(jnp.max(statR[0], axis=0))
    match[...] = (dots[...] * jnp.exp(mine - peak)).astype(BF16)

    def patches(t):
        return jnp.concatenate([t[0:PDIM], t[PDIM:W]], axis=1)

    def twice(t):
        return jnp.concatenate([t, t], axis=1)

    s = twice(sigma)
    var = s * s + SIGMA_DATA * SIGMA_DATA
    c_skip = SIGMA_DATA * SIGMA_DATA / var
    c_out = s * SIGMA_DATA / jnp.sqrt(var)
    c_in = 1.0 / jnp.sqrt(var)
    c_noise = jnp.log(s) / 4.0

    def forward(t):
        if t == 0:
            tell(1, jnp.sum(match[...].astype(F32), axis=1, keepdims=True))
            w_in_copy.wait()
            w_out_copy.wait()
        elif t == 1:
            x_full = patches(noisy[own].astype(F32).T)
            scaled = (c_in * x_full).astype(BF16)
            scaled_ref[...] = scaled
            fit_ref[...] = c_skip * x_full / c_out
            slope_ref[...] = (tn(w_in_ref[...], scaled) + column(w_noise_ref[...].reshape(1, HID)) * c_noise
                              + column(bias_ref[...].reshape(1, HID)))
        elif t == 2:
            pre = slope_ref[...]
            sig_p = jax.nn.sigmoid(pre)
            hidden_ref[...] = (pre * sig_p).astype(BF16)
            slope_ref[...] = sig_p * (1.0 + pre * (1.0 - sig_p))
        else:
            fit_ref[...] += nn(w_outT_ref[...], hidden_ref[...])

    top, bottom = reduce_scatter(forward)
    shareS[0:NA] = top
    shareS[NA:Q] = bottom
    hear(1)
    total = jnp.sum(statR[1], axis=0)

    resid = fit_ref[...] - patches(shareS[...].T / total) / c_out
    g_b = (2.0 / NQ * resid).astype(BF16)

    def strips(at_row, value):
        rows = value.shape[0]
        for h in range(2):
            for k in range(3):
                cols = slice(h * W + k * 128, h * W + k * 128 + 128)
                grads[h, at_row + k * rows:at_row + (k + 1) * rows] = value[:, cols]

    def core_copy(i):
        rows = (pl.ds(0, P_ROWS), pl.ds(P_ROWS, Z * RP))[i]
        return rcopy(grads.at[1 - core, rows], coreR.at[rows], core_ss.at[i], core_rs.at[i], sib)

    def loop(first, last, body):
        def one(k, _):
            body(k)
            return 0

        lax.fori_loop(first, last, one, 0)

    def plane_copy(src, dst, ssem, rsem, p):
        return pltpu.make_async_remote_copy(
            src_ref=src, dst_ref=dst, send_sem=ssem, recv_sem=rsem, device_id=in_plane(p), device_id_type=MESH)

    def z_copy(src, dst, ssem, rsem, o):
        return rcopy(src, dst, ssem, rsem, at(xl, o, core))

    x = me // 4

    def pp(k):
        p = (me + k) % PLANE
        return plane_copy(pS.at[p], pR.at[k], pp_ss.at[k], pp_rs.at[k], p)

    def rz(k):
        o = (z + k) % Z
        return z_copy(rS.at[o], rR.at[k], rz_ss.at[k], rz_rs.at[k], o)

    def pz(k, origin):
        view = pzR.at[origin]
        return z_copy(view, view, pz_ss.at[k], pz_rs.at[origin], (z + k) % Z)

    def rx(k, origin):
        view = rxR.at[origin]
        return plane_copy(view, view, rx_ss.at[k], rx_rs.at[origin], ((x + k) % 4) * 4 + y)

    def ry(k, origin):
        view = ryR.at[origin]
        return plane_copy(view, view, ry_ss.at[k], ry_rs.at[origin], x * 4 + (y + k) % 4)

    def pshare(k, p):
        view = wholeP.at[core, p]
        return plane_copy(view, view, pshare_ss.at[k], pshare_rs.at[p], (me + k) % PLANE)

    def rshare(k, o):
        view = wholeR.at[core, o]
        return z_copy(view, view, rshare_ss.at[k], rshare_rs.at[o], (z + k) % Z)

    def ptrade(h, p):
        return rcopy(wholeP.at[h, p], wholeP.at[h, p], trade_ss.at[p], trade_rs.at[p], sib)

    def rtrade(h, o):
        return rcopy(wholeR.at[h, o], wholeR.at[h, o], trade_ss.at[PLANE + o], trade_rs.at[PLANE + o], sib)

    strips(0, nt(g_b, hidden_ref[...]))
    dpre = tn(w_outT_ref[...], g_b) * slope_ref[...]
    strips(3 * PDIM, nt(scaled_ref[...], dpre.astype(BF16)))
    core_copy(0).start()
    objective = jnp.sum(resid * resid) / NQ
    rows = lax.broadcasted_iota(jnp.int32, (8, 2 * Q), 0)
    pick = jnp.where(rows == 0, 1.0, jnp.where(rows == 1, c_noise, 0.0))
    small = nt(pick, dpre, precision=lax.Precision.HIGHEST)
    strips(6 * PDIM, jnp.where(lax.broadcasted_iota(jnp.int32, (8, HID), 0) == 2, objective, small))
    for h in range(2):
        grads[h, 6 * PDIM + 24:] = jnp.zeros((ROWS - 6 * PDIM - 24, 128), F32)
    core_copy(1).start()
    core_copy(0).wait_recv()
    pS[...] = (grads[core, 0:P_ROWS] + coreR[0:P_ROWS]).reshape(PLANE, PP, 128)
    loop(1, PLANE, lambda k: pp(k).start())
    core_copy(1).wait_recv()
    rS[...] = (grads[core, P_ROWS:] + coreR[P_ROWS:]).reshape(Z, RP, 128)
    loop(1, Z, lambda k: rz(k).start())

    pR[0] = pS[me]

    def add_pp(k):
        pp(k).wait_recv()
        pR[0] += pR[k]

    loop(1, PLANE, add_pp)
    pzR[z] = pR[0]
    loop(1, Z, lambda k: pz(k, z).start())
    rR[0] = rS[z]

    def add_rz(k):
        rz(k).wait_recv()
        rR[0] += rR[k]

    loop(1, Z, add_rz)
    rxR[x] = rR[0]
    loop(1, 4, lambda k: rx(k, x).start())
    loop(1, 4, lambda k: rx(k, (x + k) % 4).wait_recv())
    ryR[y] = jnp.sum(rxR[...], axis=0)
    loop(1, 4, lambda k: ry(k, y).start())
    loop(1, Z, lambda k: pz(k, (z + k) % Z).wait_recv())
    wholeP[core, me] = jnp.sum(pzR[...], axis=0)
    loop(1, PLANE, lambda k: pshare(k, me).start())
    loop(1, 4, lambda k: ry(k, (y + k) % 4).wait_recv())
    wholeR[core, z] = jnp.sum(ryR[...], axis=0)
    loop(1, Z, lambda k: rshare(k, z).start())
    ptrade(core, me).start()
    rtrade(core, z).start()

    def pass_r(k):
        o = (z + Z - k) % Z
        rshare(k, o).wait_recv()
        rtrade(core, o).start()

    def pass_p(k):
        p = (me + PLANE - k) % PLANE
        pshare(k, p).wait_recv()
        ptrade(core, p).start()

    loop(1, Z, pass_r)
    loop(1, PLANE, pass_p)
    loop(0, Z, lambda o: rtrade(1 - core, o).wait_recv())
    loop(0, PLANE, lambda p: ptrade(1 - core, p).wait_recv())
    for h in range(2):
        first = wholeP[h].reshape(P_ROWS, 128)
        second = wholeR[h].reshape(Z * RP, 128)
        for k in range(3):
            cols = slice(h * W + k * 128, h * W + k * 128 + 128)
            g_outT_ref[:, cols] = first[k * PDIM:(k + 1) * PDIM]
            g_in_ref[:, cols] = first[3 * PDIM:] if k == 0 else second[(k - 1) * PDIM:k * PDIM]
            small_ref[:, cols] = second[2 * PDIM + 8 * k:2 * PDIM + 8 * k + 8]

    for i in range(2):
        core_copy(i).wait_send()
    loop(0, PLANE, lambda p: ptrade(core, p).wait_send())
    loop(0, Z, lambda o: rtrade(core, o).wait_send())

    def plane_sent(k):
        pp(k).wait_send()
        pshare(k, me).wait_send()

    def z_sent(k):
        rz(k).wait_send()
        pz(k, z).wait_send()
        rshare(k, z).wait_send()

    def side_sent(k):
        rx(k, x).wait_send()
        ry(k, y).wait_send()

    loop(1, PLANE, plane_sent)
    loop(1, Z, z_sent)
    loop(1, 4, side_sent)
    for wait in sent:
        wait()


def main_call(noise, refs, level, ids, w_in, bias, w_noise, w_outT):
    dma = pltpu.SemaphoreType.DMA
    vm = pltpu.VMEM
    any_spec = pl.BlockSpec(memory_space=pl.ANY)
    vmem_spec = pl.BlockSpec(memory_space=pltpu.VMEM)
    return pl.pallas_call(
        main_kernel,
        out_shape=[
            jax.ShapeDtypeStruct((PDIM, HID), F32),
            jax.ShapeDtypeStruct((PDIM, HID), F32),
            jax.ShapeDtypeStruct((8, HID), F32),
        ],
        in_specs=[any_spec] * 2 + [vmem_spec] * 2 + [any_spec, vmem_spec, vmem_spec, any_spec],
        out_specs=[vmem_spec] * 3,
        scratch_shapes=[
            vm((2, ROWS, 128), F32),
            vm((ROWS, 128), F32),
            vm((PLANE, PP, 128), F32),
            vm((PLANE, PP, 128), F32),
            vm((Z, PP, 128), F32),
            vm((Z, RP, 128), F32),
            vm((Z, RP, 128), F32),
            vm((4, RP, 128), F32),
            vm((4, RP, 128), F32),
            vm((2, PLANE, PP, 128), F32),
            vm((2, Z, RP, 128), F32),
            vm((PDIM, HID), BF16),
            vm((PDIM, HID), BF16),
            vm((PDIM, 2 * Q), BF16),
            vm((HID, 2 * Q), F32),
            vm((HID, 2 * Q), BF16),
            vm((PDIM, 2 * Q), F32),
            vm((2 * Z, PAIR, W), BF16),
            vm((2 * Z, Q, W), F32),
            vm((Q, PAIR), BF16),
            vm((2 * Z, Q, W), BF16),
            vm((Q, W), BF16),
            vm((Q, PAIR), F32),
            vm((Q, PAIR), F32),
            vm((Q, PAIR), F32),
            vm((2, 1, Q), F32),
            vm((2, CHIPS, 1, Q), F32),
            vm((PAIR, 128), F32),
            vm((2, Z, HALF, W), BF16),
            vm((2, Z, HALF, W), BF16),
            vm((2, 4, Q, W), BF16),
            vm((2, 4, Q, W), BF16),
            vm((1, Q), jnp.int32),
            vm((Q, PAIR), BF16),
            vm((Z, NA, W), BF16),
            vm((Z, NA, W), BF16),
            vm((2, 4, NA, W), BF16),
            vm((2, 4, NA, W), BF16),
            vm((2, 4, 2, NB, W), BF16),
            vm((2, 4, 2, NB, W), BF16),
            vm((NB, W), BF16),
            vm((NB, W), BF16),
            vm((Q, W), F32),
            dma((2 * Z + 3,)), dma((2 * Z,)), dma((2 * Z,)), dma((2,)),
            dma((2, CHIPS)), dma((2, CHIPS)),
            dma((2, Z)), dma((2, Z)), dma((2, 4, 2)), dma((2, 4, 2)), dma((2,)),
            dma((Z,)), dma((Z,)), dma((2, 4)), dma((2, 4)),
            dma((2, 4, 2)), dma((2, 4, 2)), dma((1,)), dma((1,)),
            dma((Z,)), dma((Z,)), dma((2, 4)), dma((2, 4)),
            dma((2, 4, 2)), dma((2, 4, 2)), dma((1,)), dma((1,)),
            dma((2,)), dma((2,)), dma((PLANE,)), dma((PLANE,)), dma((Z,)), dma((Z,)),
            dma((Z,)), dma((Z,)), dma((4,)), dma((4,)), dma((4,)), dma((4,)),
            dma((PLANE,)), dma((PLANE,)), dma((Z,)), dma((Z,)), dma((PLANE + Z,)), dma((PLANE + Z,)),
        ],
        compiler_params=pltpu.CompilerParams(
            collective_id=0, has_side_effects=True, vmem_limit_bytes=56 * 1024 * 1024),
        name="denoise_step",
    )(noise, refs, level, ids, w_in, bias, w_noise, w_outT)


def write_kernel(g_in_ref, g_outT_ref, small_ref, g_in_out, g_outT_out, bias_out, noise_out, loss_out):
    g_in_out[...] = g_in_ref[...]
    g_outT_out[...] = g_outT_ref[...]
    bias_out[...] = small_ref[0]
    noise_out[...] = small_ref[1]
    loss_out[...] = small_ref[2:3, 0:1] * (1.0 / FEATS)


def write_call(g_in, g_outT, small):
    vmem_spec = pl.BlockSpec(memory_space=pltpu.VMEM)
    shape = jax.ShapeDtypeStruct
    return pl.pallas_call(
        write_kernel,
        out_shape=[shape((PDIM, HID), F32)] * 2 + [shape((HID,), F32)] * 2 + [shape((1, 1), F32)],
        in_specs=[vmem_spec] * 3,
        out_specs=[vmem_spec] * 5,
        name="write_results",
    )(g_in, g_outT, small)


def per_device(noise_field, ref_crops, level_index, query_ids, w_in, bias_hidden, w_noise, w_out):
    g_in, g_outT, small = main_call(
        noise_field, ref_crops, level_index.reshape(1, Q), query_ids.reshape(1, Q), w_in,
        bias_hidden, w_noise, w_out.T)
    g_in, g_outT, bias, w_noise, loss = write_call(g_in, g_outT, small)
    return (g_in, g_outT.T, bias, w_noise, loss.reshape(()))


def solution(mesh):
    return jax.shard_map(
        per_device,
        mesh=mesh,
        in_specs=(P("query", None), P("ref", None), P("query"), P("query"), P(), P(), P(), P()),
        out_specs=(P(), P(), P(), P(), P()),
        check_vma=False,
    )
```

```python
import jax
import jax.numpy as jnp
from jax import lax
from jax.experimental import pallas as pl
from jax.experimental.pallas import tpu as pltpu
from jax.sharding import PartitionSpec as P

NLEV = 32
SIGMA_DATA = 0.5
MESH = pl.DeviceIdType.MESH
F32 = jnp.float32
BF16 = jnp.bfloat16

Z = 8
CHIPS = 2 * Z
Q = 256
HALF = 128
NA = 160
NB = Q - NA
NA0 = 80
REF = 288
PAIR = 2 * REF
W = 384
PDIM = 192
HID = 768
NQ = 2048
FEATS = 12288
PLANE = 16
PP = 48
RP = 64
P_ROWS = PLANE * PP
ROWS = P_ROWS + Z * RP


def nt(a, b, **kw):
    return lax.dot_general(a, b, (((1,), (1,)), ((), ())), preferred_element_type=F32, **kw)


def tn(a, b, **kw):
    return lax.dot_general(a, b, (((0,), (0,)), ((), ())), preferred_element_type=F32, **kw)


def nn(a, b):
    return jnp.dot(a, b, preferred_element_type=F32)


def noise_level(index):
    low = 0.05 ** (1.0 / 7.0)
    high = 80.0 ** (1.0 / 7.0)
    frac = index.astype(F32) / (NLEV - 1)
    base = high + frac * (low - high)
    two = base * base
    return two * two * two * base


def column(row):
    return jnp.broadcast_to(row, (128, row.shape[1])).T[:, 0:1]


def row_of(col):
    return jnp.broadcast_to(col, (col.shape[0], 128)).T[0:8]


def main_kernel(
    noise_hbm, refs_hbm, level_ref, ids_ref, w_in_hbm, bias_ref, w_noise_ref, w_outT_hbm,
    g_in_ref, g_outT_ref, small_ref,
    grads, coreR, pS, pR, pzR, rS, rR, rxR, ryR, wholeP, wholeR,
    w_in_ref, w_outT_ref, scaled_ref, slope_ref, hidden_ref, fit_ref,
    refs, prod, match, noisy, noise, dots, halfS, halfR, statS, statR, sqacc,
    xS, xR, zS, zR2, idsR, match2,
    axS, axR, azS, azR, bzS, bzR, bxS, bxR, shareS,
    local_sem, swap_ss, swap_rs, half_sem, stat_ss, stat_rs,
    x_ss, x_rs, zz_ss, zz_rs, ids_sem,
    ax_ss, ax_rs, az_ss, az_rs, bz_ss, bz_rs, bx_ss, bx_rs,
    gax_ss, gax_rs, gaz_ss, gaz_rs, gbz_ss, gbz_rs, gbx_ss, gbx_rs,
    core_ss, core_rs, pp_ss, pp_rs, rz_ss, rz_rs, pz_ss, pz_rs, rx_ss, rx_rs, ry_ss, ry_rs,
    pshare_ss, pshare_rs, rshare_ss, rshare_rs, trade_ss, trade_rs,
):
    q = lax.axis_index("query")
    r = lax.axis_index("ref")
    core = r % 2
    chip = r // 2
    z = chip % Z
    xl = chip // Z
    other = 1 - xl

    def at(x_at, z_at, core_at):
        return (x_at * Z + z_at) * 2 + core_at

    x_hi = q // 4
    y = q % 4
    me = (x_hi * 2 + xl) * 4 + y

    def in_plane(p):
        return ((p // 8) * 4 + p % 4, at((p // 4) % 2, z, core))

    sib = at(xl, z, 1 - core)
    xn = at(other, z, core)
    to = (at(xl, (z + Z - 1) % Z, core), at(xl, (z + 1) % Z, core))

    def rcopy(src, dst, ssem, rsem, target):
        return pltpu.make_async_remote_copy(
            src_ref=src, dst_ref=dst, send_sem=ssem, recv_sem=rsem,
            device_id=(q, target), device_id_type=MESH)

    def order(i):
        d = 4 - (i + 1) // 2
        return (z + Z + d * (2 * (i % 2) - 1)) % Z

    def local_copy(b):
        off = pl.multiple_of(core * (FEATS // 2) + b * W, 128)
        return pltpu.make_async_copy(
            refs_hbm.at[:, pl.ds(off, W)], refs.at[b, pl.ds(core * REF, REF), :], local_sem.at[b])

    def swap_copy(b):
        off = pl.multiple_of((1 - core) * (FEATS // 2) + b * W, 128)
        return rcopy(
            refs_hbm.at[:, pl.ds(off, W)], refs.at[b, pl.ds(core * REF, REF), :],
            swap_ss.at[b], swap_rs.at[b], sib)

    def swap_landed(b):
        return rcopy(
            refs_hbm.at[:, pl.ds(0, W)], refs.at[b, pl.ds((1 - core) * REF, REF), :],
            swap_ss.at[b], swap_rs.at[b], sib)

    own = 2 * z + xl

    def start_local(i, _):
        o = order(i)
        local_copy(2 * o).start()
        local_copy(2 * o + 1).start()
        return 0

    lax.fori_loop(0, Z, start_local, 0)
    noise_off = pl.multiple_of(core * (FEATS // 2) + own * W, 128)
    noise_copy = pltpu.make_async_copy(
        noise_hbm.at[:, pl.ds(noise_off, W)], noise, local_sem.at[2 * Z])
    noise_copy.start()
    w_in_copy = pltpu.make_async_copy(w_in_hbm, w_in_ref, local_sem.at[2 * Z + 1])
    w_out_copy = pltpu.make_async_copy(w_outT_hbm, w_outT_ref, local_sem.at[2 * Z + 2])
    w_in_copy.start()
    w_out_copy.start()

    barrier = pltpu.get_barrier_semaphore()

    def greet(k, _):
        peer = (chip + k) % CHIPS
        pl.semaphore_signal(barrier, inc=1, device_id=(q, peer * 2 + core), device_id_type=MESH)
        return 0

    lax.fori_loop(1, CHIPS, greet, 0)
    pl.semaphore_signal(barrier, inc=1, device_id=(q, sib), device_id_type=MESH)

    def greet_plane(k, _):
        p = (me + k) % PLANE

        @pl.when(p != x_peer)
        def _():
            pl.semaphore_signal(barrier, inc=1, device_id=in_plane(p), device_id_type=MESH)

        return 0

    x_peer = (x_hi * 2 + other) * 4 + y
    lax.fori_loop(1, PLANE, greet_plane, 0)
    pl.semaphore_wait(barrier, CHIPS + PLANE - 2)

    sent = []

    def start_swap(i):
        o = order(i)
        swap_copy(2 * o).start()
        swap_copy(2 * o + 1).start()

    xo = at(other, z, core)
    q_xo = (1 - x_hi) * 4 + y
    ids_copy = pltpu.make_async_remote_copy(
        src_ref=ids_ref, dst_ref=idsR, send_sem=ids_sem.at[0], recv_sem=ids_sem.at[1],
        device_id=(q_xo, xo), device_id_type=MESH)
    ids_copy.start()
    sent.append(ids_copy.wait_send)
    for i in range(3):
        start_swap(i)

    def swap_sent():
        def one(b, _):
            swap_copy(b).wait_send()
            return 0

        lax.fori_loop(0, 2 * Z, one, 0)

    sent.append(swap_sent)

    sigma = noise_level(level_ref[...])
    sigma_col = column(sigma)
    places = lax.broadcasted_iota(jnp.int32, (Q, PAIR), 1).astype(F32)

    def one_hot(row):
        ids = column(row.astype(F32)) - (chip * PAIR).astype(F32)
        return (ids == places).astype(F32).astype(BF16)

    match[...] = one_hot(ids_ref[...])
    match2[0:HALF] = match[0:HALF]

    def x_copy(side, o):
        return pltpu.make_async_remote_copy(
            src_ref=xS.at[side, o], dst_ref=xR.at[side, o], send_sem=x_ss.at[side, o], recv_sem=x_rs.at[side, o],
            device_id=(q if side == 0 else q_xo, xn), device_id_type=MESH)

    def z_step(d, t, side):
        rows = pl.ds(HALF * side, HALF)
        return rcopy(zS.at[d, t, rows], zR2.at[d, t, rows], zz_ss.at[d, t, side], zz_rs.at[d, t, side], to[d])

    def first_multiply(i):
        o = order(i)
        if i + 3 < Z:
            start_swap(i + 3)
        for j in range(2):
            local_copy(2 * o + j).wait()
            swap_landed(2 * o + j).wait_recv()
        part = nn(match2[...], refs[2 * o + other]).astype(BF16)
        for side in range(2):
            xS[side, o] = part[side * HALF:(side + 1) * HALF]
            x_copy(side, o).start()
        prod[2 * o + xl] = nn(match[...], refs[2 * o + xl])

    def first_sum(o, side):
        x_copy(side, o).wait_recv()
        return prod[2 * o + xl, side * HALF:(side + 1) * HALF] + xR[side, o].astype(F32)

    def toward(d, t):
        return (z + Z + (2 * d - 1) * (4 - t)) % Z

    def opposite(d):
        return pl.ds(NA0 * d, (NA0, NA - NA0)[d])

    def first_reduce(idle):
        for i in range(3):
            first_multiply(i)
        for d in range(2):
            zS[d, 0, d * HALF:(d + 1) * HALF] = first_sum(toward(d, 0), d).astype(BF16)
            z_step(d, 0, d).start()
        for t in range(1, 4):
            for i in range(2 * t + 1, min(2 * t + 3, Z)):
                first_multiply(i)
            idle(t)
            for side in range(2):
                rows = slice(side * HALF, (side + 1) * HALF)
                for d in range(2):
                    part = first_sum(toward(d, t), side)
                    if t > 1 or side == d:
                        z_step(d, t - 1, side).wait_recv()
                        part = part + zR2[d, t - 1, rows].astype(F32)
                    zS[d, t, rows] = part.astype(BF16)
                    z_step(d, t, side).start()
        idle(0)
        parts = [first_sum(z, side) for side in range(2)]
        for side in range(2):
            for d in range(2):
                z_step(d, 3, side).wait_recv()
                parts[side] = parts[side] + zR2[d, 3, side * HALF:(side + 1) * HALF].astype(F32)

        def finish():
            for d in range(2):
                z_step(d, 0, d).wait_send()
                for t in range(1, 4):
                    for side in range(2):
                        z_step(d, t, side).wait_send()

            def one(o, _):
                x_copy(0, o).wait_send()
                x_copy(1, o).wait_send()
                return 0

            lax.fori_loop(0, Z, one, 0)

        sent.append(finish)
        return parts

    def reduce_scatter(idle):
        def ax(o):
            return rcopy(axS.at[o], axR.at[o], ax_ss.at[o], ax_rs.at[o], xn)

        def az(d, t, h):
            rows = opposite(h)
            return rcopy(azS.at[d, t, rows], azR.at[d, t, rows], az_ss.at[d, t, h], az_rs.at[d, t, h], to[d])

        def bz(d, t, j):
            return rcopy(bzS.at[d, t, j], bzR.at[d, t, j], bz_ss.at[d, t, j], bz_rs.at[d, t, j], to[d])

        def bx():
            return rcopy(bxS, bxR, bx_ss.at[0], bx_rs.at[0], xn)

        def multiply(i):
            o = order(i)
            for j in range(2):
                prod[2 * o + j] = nn(match[...], refs[2 * o + j])
            axS[o] = prod[2 * o + other, 0:NA].astype(BF16)
            ax(o).start()

        multiply(0)
        for d in range(2):
            bzS[d, 0, d] = prod[2 * toward(d, 0) + d, NA:Q].astype(BF16)
            bz(d, 0, d).start()
        multiply(1)
        multiply(2)
        idle(0)
        o = toward(0, 0)
        ax(o).wait_recv()
        for d in range(2):
            rows = opposite(d)
            azS[d, 0, rows] = (prod[2 * o + xl, rows] + axR[o, rows].astype(F32)).astype(BF16)
            az(d, 0, d).start()
        for t in range(1, 4):
            for j in range(2):
                for d in range(2):
                    s = prod[2 * toward(d, t) + j, NA:Q]
                    if t > 1 or j == d:
                        bz(d, t - 1, j).wait_recv()
                        s = s + bzR[d, t - 1, j].astype(F32)
                    bzS[d, t, j] = s.astype(BF16)
                    bz(d, t, j).start()
            for i in range(2 * t + 1, min(2 * t + 3, Z)):
                multiply(i)
            for d in range(2):
                ax(toward(d, t)).wait_recv()
            for h in range(2):
                for d in range(2):
                    o = toward(d, t)
                    rows = opposite(h)
                    s = prod[2 * o + xl, rows] + axR[o, rows].astype(F32)
                    if t > 1 or h == d:
                        az(d, t - 1, h).wait_recv()
                        s = s + azR[d, t - 1, rows].astype(F32)
                    azS[d, t, rows] = s.astype(BF16)
                    az(d, t, h).start()
            idle(t)
        for d in range(2):
            for j in range(2):
                bz(d, 3, j).wait_recv()
        bxS[...] = (prod[2 * z + other, NA:Q] + bzR[0, 3, other].astype(F32)
                    + bzR[1, 3, other].astype(F32)).astype(BF16)
        bx().start()
        ax(z).wait_recv()
        for d in range(2):
            for h in range(2):
                az(d, 3, h).wait_recv()
        top = (prod[own, 0:NA] + axR[z].astype(F32) + azR[0, 3].astype(F32) + azR[1, 3].astype(F32))
        bottom = prod[own, NA:Q] + bzR[0, 3, xl].astype(F32) + bzR[1, 3, xl].astype(F32)
        bx().wait_recv()
        bottom = bottom + bxR[...].astype(F32)

        def finish():
            for d in range(2):
                az(d, 0, d).wait_send()
                bz(d, 0, d).wait_send()
                for t in range(1, 4):
                    for j in range(2):
                        az(d, t, j).wait_send()
                        bz(d, t, j).wait_send()
            bx().wait_send()

            def one(o, _):
                ax(o).wait_send()
                return 0

            lax.fori_loop(0, Z, one, 0)

        sent.append(finish)
        return top, bottom

    sqacc[...] = jnp.zeros_like(sqacc)

    def squares(t):
        def one(b, _):
            v = refs[b].astype(F32)
            v = v * v
            sqacc[...] += v[:, 0:128] + v[:, 128:256] + v[:, 256:384]
            return 0

        if t == 0:
            lax.fori_loop(0, 2 * Z, one, 0)

    ids_copy.wait_recv()
    match2[HALF:Q] = one_hot(idsR[...])[HALF:Q]
    top, bottom = first_reduce(squares)
    noise_copy.wait()
    noisy[own, 0:HALF] = (top + sigma_col[0:HALF] * noise[0:HALF].astype(F32)).astype(BF16)
    noisy[own, HALF:Q] = (bottom + sigma_col[HALF:Q] * noise[HALF:Q].astype(F32)).astype(BF16)

    def same(ref, ssem, rsem, target):
        return rcopy(ref, ref, ssem, rsem, target)

    def gax(o, x_at):
        return same(noisy.at[2 * o + x_at, 0:NA], gax_ss.at[o], gax_rs.at[o], xn)

    def gbx(x_at):
        return same(noisy.at[2 * z + x_at, NA:Q], gbx_ss.at[0], gbx_rs.at[0], xn)

    def gaz(d, s, o, h):
        return same(noisy.at[2 * o + xl, opposite(h)], gaz_ss.at[d, s - 1, h], gaz_rs.at[d, s - 1, h], to[d])

    def gbz(d, s, o, j):
        return same(noisy.at[2 * o + j, NA:Q], gbz_ss.at[d, s - 1, j], gbz_rs.at[d, s - 1, j], to[d])

    def came(d, s):
        return (z + Z + (1 - 2 * d) * s) % Z

    def score(o, first=False):
        part = nt(noisy[2 * o], refs[2 * o]) + nt(noisy[2 * o + 1], refs[2 * o + 1])
        dots[...] = part if first else dots[...] + part

    gbx(xl).start()
    for h in range(2):
        for d in range(2):
            gaz(d, 1, z, h).start()
    for d in range(2):
        gbz(d, 1, z, xl).start()
    gax(z, xl).start()
    gbx(other).wait_recv()
    for d in range(2):
        gbz(d, 1, z, other).start()

    for s in range(1, 4):
        for h in range(2):
            for d in range(2):
                o = came(d, s)
                gaz(d, s, o, h).wait_recv()
                if s < 3 or h == d:
                    gaz(d, s + 1, o, h).start()
        for d in range(2):
            gax(came(d, s), xl).start()
        for j in (xl, other) if s < 3 else (0, 1):
            for d in range(2):
                o = came(d, s)
                gbz(d, s, o, j).wait_recv()
                if s < 3 or j == d:
                    gbz(d, s + 1, o, j).start()
        if s == 1:
            gax(z, other).wait_recv()
            score(z, True)
        else:
            for d in range(2):
                o = came(d, s - 1)
                gax(o, other).wait_recv()
                score(o)
    ref_sq = nt(jnp.ones((8, 128), F32), sqacc[...], precision=lax.Precision.HIGHEST)[0:1]
    o = came(0, 4)
    for d in range(2):
        gaz(d, 4, o, d).wait_recv()
    gax(o, xl).start()
    for d in range(2):
        gax(came(d, 3), other).wait_recv()
        score(came(d, 3))
    for d in range(2):
        gbz(d, 4, o, d).wait_recv()
    gax(o, other).wait_recv()
    score(o)

    def gather_sent():
        gbx(xl).wait_send()

        def one(o, _):
            gax(o, xl).wait_send()
            return 0

        lax.fori_loop(0, Z, one, 0)
        for d in range(2):
            for s in range(1, 5):
                for j in range(2):
                    if s < 4 or j == d:
                        gaz(d, s, z, j).wait_send()
                        gbz(d, s, z, j).wait_send()

    sent.append(gather_sent)

    def patches(t):
        return jnp.concatenate([t[0:PDIM], t[PDIM:W]], axis=1)

    def twice(t):
        return jnp.concatenate([t, t], axis=1)

    s = twice(sigma)
    var = s * s + SIGMA_DATA * SIGMA_DATA
    c_skip = SIGMA_DATA * SIGMA_DATA / var
    c_out = s * SIGMA_DATA / jnp.sqrt(var)
    c_in = 1.0 / jnp.sqrt(var)
    c_noise = jnp.log(s) / 4.0

    def forward(t):
        if t == 0:
            tell(1, jnp.sum(match[...].astype(F32), axis=1, keepdims=True))
        elif t == 1:
            fit_ref[...] += nn(w_outT_ref[...], hidden_ref[...])

    def before(t):
        if t == 0:
            w_in_copy.wait()
            w_out_copy.wait()
            x_full = patches(noisy[own].astype(F32).T)
            scaled = (c_in * x_full).astype(BF16)
            scaled_ref[...] = scaled
            fit_ref[...] = c_skip * x_full / c_out
            slope_ref[...] = (tn(w_in_ref[...], scaled) + column(w_noise_ref[...].reshape(1, HID)) * c_noise
                              + column(bias_ref[...].reshape(1, HID)))
        else:
            pre = slope_ref[...]
            sig_p = jax.nn.sigmoid(pre)
            hidden_ref[...] = (pre * sig_p).astype(BF16)
            slope_ref[...] = sig_p * (1.0 + pre * (1.0 - sig_p))

    halfS[...] = 2.0 * dots[...] - ref_sq
    half = rcopy(halfS, halfR, half_sem.at[0], half_sem.at[1], sib)
    half.start()
    sent.append(half.wait_send)
    before(0)
    half.wait_recv()
    logits = (halfS[...] + halfR[...]) / (2.0 * sigma_col * sigma_col)
    dots[...] = logits

    def stat(i, k):
        peer = ((chip + k) % CHIPS) * 2 + core
        return rcopy(statS.at[i], statR.at[i, k], stat_ss.at[i, k], stat_rs.at[i, k], peer)

    def tell(i, col):
        statS[i] = row_of(col)[0:1]
        statR[i, 0] = statS[i]

        def one(k, _):
            stat(i, k).start()
            return 0

        lax.fori_loop(1, CHIPS, one, 0)

        def told():
            def one(k, _):
                stat(i, k).wait_send()
                return 0

            lax.fori_loop(1, CHIPS, one, 0)

        sent.append(told)

    def hear(i):
        def one(k, _):
            stat(i, k).wait_recv()
            return 0

        lax.fori_loop(1, CHIPS, one, 0)

    mine = jnp.max(logits, axis=1, keepdims=True)
    tell(0, mine)
    dots[...] = jnp.exp(logits - mine)
    before(1)
    hear(0)
    peak = column(jnp.max(statR[0], axis=0))
    match[...] = (dots[...] * jnp.exp(mine - peak)).astype(BF16)

    top, bottom = reduce_scatter(forward)
    shareS[0:NA] = top
    shareS[NA:Q] = bottom
    hear(1)
    total = jnp.sum(statR[1], axis=0)

    resid = fit_ref[...] - patches(shareS[...].T / total) / c_out
    g_b = (2.0 / NQ * resid).astype(BF16)

    def strips(at_row, value):
        rows = value.shape[0]
        for h in range(2):
            for k in range(3):
                cols = slice(h * W + k * 128, h * W + k * 128 + 128)
                grads[h, at_row + k * rows:at_row + (k + 1) * rows] = value[:, cols]

    def core_copy(i):
        rows = (pl.ds(0, P_ROWS), pl.ds(P_ROWS, Z * RP))[i]
        return rcopy(grads.at[1 - core, rows], coreR.at[rows], core_ss.at[i], core_rs.at[i], sib)

    def loop(first, last, body):
        def one(k, _):
            body(k)
            return 0

        lax.fori_loop(first, last, one, 0)

    def plane_copy(src, dst, ssem, rsem, p):
        return pltpu.make_async_remote_copy(
            src_ref=src, dst_ref=dst, send_sem=ssem, recv_sem=rsem, device_id=in_plane(p), device_id_type=MESH)

    def z_copy(src, dst, ssem, rsem, o):
        return rcopy(src, dst, ssem, rsem, at(xl, o, core))

    x = me // 4

    def pp(k):
        p = (me + k) % PLANE
        return plane_copy(pS.at[p], pR.at[k], pp_ss.at[k], pp_rs.at[k], p)

    def rz(k):
        o = (z + k) % Z
        return z_copy(rS.at[o], rR.at[k], rz_ss.at[k], rz_rs.at[k], o)

    def pz(k, origin):
        view = pzR.at[origin]
        return z_copy(view, view, pz_ss.at[k], pz_rs.at[origin], (z + k) % Z)

    def rx(k, origin):
        view = rxR.at[origin]
        return plane_copy(view, view, rx_ss.at[k], rx_rs.at[origin], ((x + k) % 4) * 4 + y)

    def ry(k, origin):
        view = ryR.at[origin]
        return plane_copy(view, view, ry_ss.at[k], ry_rs.at[origin], x * 4 + (y + k) % 4)

    def pshare(k, p):
        view = wholeP.at[core, p]
        return plane_copy(view, view, pshare_ss.at[k], pshare_rs.at[p], (me + k) % PLANE)

    def rshare(k, o):
        view = wholeR.at[core, o]
        return z_copy(view, view, rshare_ss.at[k], rshare_rs.at[o], (z + k) % Z)

    def ptrade(h, p):
        return rcopy(wholeP.at[h, p], wholeP.at[h, p], trade_ss.at[p], trade_rs.at[p], sib)

    def rtrade(h, o):
        return rcopy(wholeR.at[h, o], wholeR.at[h, o], trade_ss.at[PLANE + o], trade_rs.at[PLANE + o], sib)

    strips(0, nt(g_b, hidden_ref[...]))
    dpre = tn(w_outT_ref[...], g_b) * slope_ref[...]
    strips(3 * PDIM, nt(scaled_ref[...], dpre.astype(BF16)))
    core_copy(0).start()
    objective = jnp.sum(resid * resid) / NQ
    rows = lax.broadcasted_iota(jnp.int32, (8, 2 * Q), 0)
    pick = jnp.where(rows == 0, 1.0, jnp.where(rows == 1, c_noise, 0.0))
    small = nt(pick, dpre, precision=lax.Precision.HIGHEST)
    strips(6 * PDIM, jnp.where(lax.broadcasted_iota(jnp.int32, (8, HID), 0) == 2, objective, small))
    for h in range(2):
        grads[h, 6 * PDIM + 24:] = jnp.zeros((ROWS - 6 * PDIM - 24, 128), F32)
    core_copy(1).start()
    core_copy(0).wait_recv()
    pS[...] = (grads[core, 0:P_ROWS] + coreR[0:P_ROWS]).reshape(PLANE, PP, 128)
    loop(1, PLANE, lambda k: pp(k).start())
    core_copy(1).wait_recv()
    rS[...] = (grads[core, P_ROWS:] + coreR[P_ROWS:]).reshape(Z, RP, 128)
    loop(1, Z, lambda k: rz(k).start())

    pR[0] = pS[me]

    def add_pp(k):
        pp(k).wait_recv()
        pR[0] += pR[k]

    loop(1, PLANE, add_pp)
    pzR[z] = pR[0]
    loop(1, Z, lambda k: pz(k, z).start())
    rR[0] = rS[z]

    def add_rz(k):
        rz(k).wait_recv()
        rR[0] += rR[k]

    loop(1, Z, add_rz)
    rxR[x] = rR[0]
    loop(1, 4, lambda k: rx(k, x).start())
    loop(1, 4, lambda k: rx(k, (x + k) % 4).wait_recv())
    ryR[y] = jnp.sum(rxR[...], axis=0)
    loop(1, 4, lambda k: ry(k, y).start())
    loop(1, Z, lambda k: pz(k, (z + k) % Z).wait_recv())
    wholeP[core, me] = jnp.sum(pzR[...], axis=0)
    loop(1, PLANE, lambda k: pshare(k, me).start())
    loop(1, 4, lambda k: ry(k, (y + k) % 4).wait_recv())
    wholeR[core, z] = jnp.sum(ryR[...], axis=0)
    loop(1, Z, lambda k: rshare(k, z).start())
    ptrade(core, me).start()
    rtrade(core, z).start()

    def pass_r(k):
        o = (z + Z - k) % Z
        rshare(k, o).wait_recv()
        rtrade(core, o).start()

    def pass_p(k):
        p = (me + PLANE - k) % PLANE
        pshare(k, p).wait_recv()
        ptrade(core, p).start()

    loop(1, Z, pass_r)
    loop(1, PLANE, pass_p)
    loop(0, Z, lambda o: rtrade(1 - core, o).wait_recv())
    loop(0, PLANE, lambda p: ptrade(1 - core, p).wait_recv())
    for h in range(2):
        first = wholeP[h].reshape(P_ROWS, 128)
        second = wholeR[h].reshape(Z * RP, 128)
        for k in range(3):
            cols = slice(h * W + k * 128, h * W + k * 128 + 128)
            g_outT_ref[:, cols] = first[k * PDIM:(k + 1) * PDIM]
            g_in_ref[:, cols] = first[3 * PDIM:] if k == 0 else second[(k - 1) * PDIM:k * PDIM]
            small_ref[:, cols] = second[2 * PDIM + 8 * k:2 * PDIM + 8 * k + 8]

    for i in range(2):
        core_copy(i).wait_send()
    loop(0, PLANE, lambda p: ptrade(core, p).wait_send())
    loop(0, Z, lambda o: rtrade(core, o).wait_send())

    def plane_sent(k):
        pp(k).wait_send()
        pshare(k, me).wait_send()

    def z_sent(k):
        rz(k).wait_send()
        pz(k, z).wait_send()
        rshare(k, z).wait_send()

    def side_sent(k):
        rx(k, x).wait_send()
        ry(k, y).wait_send()

    loop(1, PLANE, plane_sent)
    loop(1, Z, z_sent)
    loop(1, 4, side_sent)
    for wait in sent:
        wait()


def main_call(noise, refs, level, ids, w_in, bias, w_noise, w_outT):
    dma = pltpu.SemaphoreType.DMA
    vm = pltpu.VMEM
    any_spec = pl.BlockSpec(memory_space=pl.ANY)
    vmem_spec = pl.BlockSpec(memory_space=pltpu.VMEM)
    return pl.pallas_call(
        main_kernel,
        out_shape=[
            jax.ShapeDtypeStruct((PDIM, HID), F32),
            jax.ShapeDtypeStruct((PDIM, HID), F32),
            jax.ShapeDtypeStruct((8, HID), F32),
        ],
        in_specs=[any_spec] * 2 + [vmem_spec] * 2 + [any_spec, vmem_spec, vmem_spec, any_spec],
        out_specs=[vmem_spec] * 3,
        scratch_shapes=[
            vm((2, ROWS, 128), F32),
            vm((ROWS, 128), F32),
            vm((PLANE, PP, 128), F32),
            vm((PLANE, PP, 128), F32),
            vm((Z, PP, 128), F32),
            vm((Z, RP, 128), F32),
            vm((Z, RP, 128), F32),
            vm((4, RP, 128), F32),
            vm((4, RP, 128), F32),
            vm((2, PLANE, PP, 128), F32),
            vm((2, Z, RP, 128), F32),
            vm((PDIM, HID), BF16),
            vm((PDIM, HID), BF16),
            vm((PDIM, 2 * Q), BF16),
            vm((HID, 2 * Q), F32),
            vm((HID, 2 * Q), BF16),
            vm((PDIM, 2 * Q), F32),
            vm((2 * Z, PAIR, W), BF16),
            vm((2 * Z, Q, W), F32),
            vm((Q, PAIR), BF16),
            vm((2 * Z, Q, W), BF16),
            vm((Q, W), BF16),
            vm((Q, PAIR), F32),
            vm((Q, PAIR), F32),
            vm((Q, PAIR), F32),
            vm((2, 1, Q), F32),
            vm((2, CHIPS, 1, Q), F32),
            vm((PAIR, 128), F32),
            vm((2, Z, HALF, W), BF16),
            vm((2, Z, HALF, W), BF16),
            vm((2, 4, Q, W), BF16),
            vm((2, 4, Q, W), BF16),
            vm((1, Q), jnp.int32),
            vm((Q, PAIR), BF16),
            vm((Z, NA, W), BF16),
            vm((Z, NA, W), BF16),
            vm((2, 4, NA, W), BF16),
            vm((2, 4, NA, W), BF16),
            vm((2, 4, 2, NB, W), BF16),
            vm((2, 4, 2, NB, W), BF16),
            vm((NB, W), BF16),
            vm((NB, W), BF16),
            vm((Q, W), F32),
            dma((2 * Z + 3,)), dma((2 * Z,)), dma((2 * Z,)), dma((2,)),
            dma((2, CHIPS)), dma((2, CHIPS)),
            dma((2, Z)), dma((2, Z)), dma((2, 4, 2)), dma((2, 4, 2)), dma((2,)),
            dma((Z,)), dma((Z,)), dma((2, 4, 2)), dma((2, 4, 2)),
            dma((2, 4, 2)), dma((2, 4, 2)), dma((1,)), dma((1,)),
            dma((Z,)), dma((Z,)), dma((2, 4, 2)), dma((2, 4, 2)),
            dma((2, 4, 2)), dma((2, 4, 2)), dma((1,)), dma((1,)),
            dma((2,)), dma((2,)), dma((PLANE,)), dma((PLANE,)), dma((Z,)), dma((Z,)),
            dma((Z,)), dma((Z,)), dma((4,)), dma((4,)), dma((4,)), dma((4,)),
            dma((PLANE,)), dma((PLANE,)), dma((Z,)), dma((Z,)), dma((PLANE + Z,)), dma((PLANE + Z,)),
        ],
        compiler_params=pltpu.CompilerParams(
            collective_id=0, has_side_effects=True, vmem_limit_bytes=56 * 1024 * 1024),
        name="denoise_step",
    )(noise, refs, level, ids, w_in, bias, w_noise, w_outT)


def write_kernel(g_in_ref, g_outT_ref, small_ref, g_in_out, g_outT_out, bias_out, noise_out, loss_out):
    g_in_out[...] = g_in_ref[...]
    g_outT_out[...] = g_outT_ref[...]
    bias_out[...] = small_ref[0]
    noise_out[...] = small_ref[1]
    loss_out[...] = small_ref[2:3, 0:1] * (1.0 / FEATS)


def write_call(g_in, g_outT, small):
    vmem_spec = pl.BlockSpec(memory_space=pltpu.VMEM)
    shape = jax.ShapeDtypeStruct
    return pl.pallas_call(
        write_kernel,
        out_shape=[shape((PDIM, HID), F32)] * 2 + [shape((HID,), F32)] * 2 + [shape((1, 1), F32)],
        in_specs=[vmem_spec] * 3,
        out_specs=[vmem_spec] * 5,
        name="write_results",
    )(g_in, g_outT, small)


def per_device(noise_field, ref_crops, level_index, query_ids, w_in, bias_hidden, w_noise, w_out):
    g_in, g_outT, small = main_call(
        noise_field, ref_crops, level_index.reshape(1, Q), query_ids.reshape(1, Q), w_in,
        bias_hidden, w_noise, w_out.T)
    g_in, g_outT, bias, w_noise, loss = write_call(g_in, g_outT, small)
    return (g_in, g_outT.T, bias, w_noise, loss.reshape(()))


def solution(mesh):
    return jax.shard_map(
        per_device,
        mesh=mesh,
        in_specs=(P("query", None), P("ref", None), P("query"), P("query"), P(), P(), P(), P()),
        out_specs=(P(), P(), P(), P(), P()),
        check_vma=False,
    )
```
